512 devices in a mesh: items: 32 (over x, y), users: 16 (over z, core).
Axes of the slice: x: 4, y: 8, z: 8, core: 2. Of those that a mesh axis runs over, the one named last changes fastest.
Arguments:
- user_vectors: float32 [8192, 256], P('users'), may hold values from -64 to 64
- item_vectors: float32 [16384, 256], P(('items', 'users')), may hold values from -1 to 1
- item_counts: int32 [16384], P(('items', 'users')), may hold values from 0 to 1048575
- positive_ids: int32 [8192], P('users'), may hold values from 0 to 16383
Outputs:
- user_loss: float32 [8192], P('users')
- user_grad: float32 [8192, 256], P('users')
- item_grad: float32 [16384, 256], P(('items', 'users'))
The draws below stay inside these ranges and needn't reach their ends.
All inputs are finite; a program needn't handle non-finite values.
Results may differ from the reference program's by a relative error of at most 0.0025.
Values sent between devices are 32-bit elements; how exact they have to be, the bound alone decides.
No kernel may reach another device: no remote copies, remote signals or barrier semaphores. Data moves between devices by JAX's collectives and lax.ppermute only.
A program may use at most 128 MiB of HBM per device.

```python
import math
import jax
import jax.numpy as jnp
from jax import lax

E = 256
ITEMS = 16384
USERS = 8192


def shared_bank(key):
    count_key = jax.random.fold_in(key, 101)
    shift_key = jax.random.fold_in(key, 102)
    bank_key = jax.random.fold_in(key, 103)
    place_key = jax.random.fold_in(key, 104)
    raw_counts = jax.random.randint(count_key, (ITEMS,), 0, 1048576, dtype=jnp.int32)
    shifts = jax.random.randint(shift_key, (ITEMS,), 0, 20, dtype=jnp.int32)
    counts = jnp.right_shift(raw_counts, shifts)
    top_place = jax.random.randint(place_key, (), 0, ITEMS, dtype=jnp.int32)
    low_place = (top_place + ITEMS // 2) % ITEMS
    positions = jnp.arange(ITEMS, dtype=jnp.int32)
    counts = jnp.where(positions == top_place, 1048575, counts)
    counts = jnp.where(positions == low_place, 0, counts)
    normal_bank = jnp.clip(jax.random.normal(bank_key, (ITEMS, E), jnp.float32), -6.0, 6.0) / math.sqrt(E)
    return (counts, normal_bank)


def draw_item_counts(key, part):
    counts, normal_bank = shared_bank(key)
    return counts


def draw_item_vectors(key, part):
    counts, normal_bank = shared_bank(key)
    return normal_bank


def draw_user_vectors(key, part):
    key = jax.random.fold_in(key, 7)
    return 3.0 * jnp.clip(jax.random.normal(jax.random.fold_in(key, 5), (USERS, E), jnp.float32), -8.0, 8.0)


def touch_ends(result, own_key, least, top_value):
    place = [jax.random.randint(jax.random.fold_in(own_key, axis), (), 0, length) for axis, length in enumerate(result.shape)]
    longest = result.shape.index(max(result.shape))
    beside = place[:longest] + [(place[longest] + 1) % result.shape[longest]] + place[longest + 1:]
    return result.at[tuple(place)].set(least).at[tuple(beside)].set(top_value)


def setup_inputs(seed: int = 0) -> dict:
    arg_keys = jax.random.split(jax.random.key(seed), 5)
    return {
        "user_vectors": draw_user_vectors(jax.random.fold_in(arg_keys[4], 71), 0),
        "item_vectors": draw_item_vectors(jax.random.fold_in(arg_keys[4], 71), 0),
        "item_counts": draw_item_counts(jax.random.fold_in(arg_keys[4], 71), 0),
        "positive_ids": touch_ends(jax.random.randint(arg_keys[3], (USERS,), 0, ITEMS), jax.random.fold_in(arg_keys[3], 1), 0, ITEMS - 1).astype(jnp.int32),
    }


HIGH = lax.Precision.HIGHEST

def block_scores(user_vectors, item_block, prior_block):
    return jnp.dot(user_vectors, item_block.T, precision=HIGH, preferred_element_type=jnp.float32) - prior_block[None, :]

def reference(user_vectors, item_vectors, item_counts, positive_ids):
    priors = jnp.log1p(item_counts.astype(jnp.float32))
    block_rows = math.gcd(ITEMS, 4096)
    count_blocks = ITEMS // block_rows
    items_blocked = item_vectors.reshape(count_blocks, block_rows, E)
    priors_blocked = priors.reshape(count_blocks, block_rows)

    def online(carried, inputs):
        highest, exp_total, weighted = carried
        item_block, prior_block = inputs
        scores = block_scores(user_vectors, item_block, prior_block)
        new_highest = jnp.maximum(highest, lax.optimization_barrier(jnp.max(scores, axis=1)))
        factor = jnp.exp(highest - new_highest)
        exponent_terms = jnp.exp(scores - new_highest[:, None])
        exp_total = exp_total * factor + lax.optimization_barrier(jnp.sum(exponent_terms, axis=1))
        weighted = weighted * factor[:, None] + jnp.dot(exponent_terms, item_block, precision=HIGH, preferred_element_type=jnp.float32)
        return ((new_highest, exp_total, weighted), None)
    starting = (jnp.full((USERS,), -jnp.inf, jnp.float32), jnp.zeros((USERS,), jnp.float32), jnp.zeros((USERS, E), jnp.float32))
    (highest, exp_total, weighted), _ = lax.scan(online, starting, (items_blocked, priors_blocked))
    log_total = highest + jnp.log(exp_total)
    positive_rows = jnp.take(item_vectors, positive_ids, axis=0)
    positive_score = lax.optimization_barrier(jnp.sum(user_vectors * positive_rows, axis=1)) - jnp.take(priors, positive_ids, axis=0)
    user_loss = log_total - positive_score
    user_grad = weighted / exp_total[:, None] - positive_rows

    def block_grad(inputs):
        item_block, prior_block, first_row = inputs
        scores = block_scores(user_vectors, item_block, prior_block)
        probability = jnp.exp(scores - log_total[:, None])
        item_ids = first_row + jnp.arange(block_rows, dtype=jnp.int32)
        target = (positive_ids[:, None] == item_ids[None, :]).astype(jnp.float32)
        return jnp.dot((probability - target).T, user_vectors, precision=HIGH, preferred_element_type=jnp.float32)
    firsts = jnp.arange(count_blocks, dtype=jnp.int32) * block_rows
    item_grad = lax.map(block_grad, (items_blocked, priors_blocked, firsts)).reshape(ITEMS, E)
    return (user_loss, user_grad, item_grad)
```

```python
import functools

import jax
import jax.numpy as jnp
from jax import lax
from jax.experimental import pallas as pl
from jax.experimental.pallas import tpu as pltpu
from jax.sharding import PartitionSpec as P

HIGH = lax.Precision.HIGHEST
GROUPS, MEMBERS = 32, 16
Z, CORES = 8, 2
E = 256
OWN = 32
PACK = OWN + 8
SLAB = MEMBERS * OWN
HALF = SLAB // CORES
ROWS = 512
SHARE = ROWS // GROUPS
SENT = 4 * SHARE + 8
VMEM_LIMIT = 48 * 1024 * 1024


def vmem():
    return pl.BlockSpec(memory_space=pltpu.VMEM)


def smem():
    return pl.BlockSpec(memory_space=pltpu.SMEM)


def f32(*shape):
    return jax.ShapeDtypeStruct(shape, jnp.float32)


def call(body, out_shape, operands, scalars=0, scratch=(), flops=0):
    single = not isinstance(out_shape, (tuple, list))
    outs = [out_shape] if single else list(out_shape)
    size = sum(o.size * 4 for o in operands) + sum(4 * s.size for s in outs)
    result = pl.pallas_call(
        body,
        out_shape=outs,
        in_specs=[smem()] * scalars + [vmem()] * (len(operands) - scalars),
        out_specs=[vmem()] * len(outs),
        scratch_shapes=list(scratch),
        compiler_params=pltpu.CompilerParams(vmem_limit_bytes=VMEM_LIMIT),
        cost_estimate=pl.CostEstimate(flops=flops, bytes_accessed=size, transcendentals=0),
    )(*operands)
    return result[0] if single else result


def dot(a, b, contract_a, contract_b):
    return lax.dot_general(
        a, b, (((contract_a,), (contract_b,)), ((), ())),
        precision=HIGH, preferred_element_type=jnp.float32,
    )


def pack_body(items, counts, out):
    out[0:OWN, :] = items[...]
    priors = jnp.log(1.0 + counts[...].astype(jnp.float32))
    out[OWN:PACK, :] = jnp.zeros((PACK - OWN, E), jnp.float32)
    out[OWN:OWN + 1, 0:OWN] = priors


def column_of(row):
    size = row.shape[1]
    eye = lax.broadcasted_iota(jnp.int32, (size, size), 0) == lax.broadcasted_iota(
        jnp.int32, (size, size), 1
    )
    return jnp.sum(jnp.where(eye, jnp.broadcast_to(row, (size, size)), 0.0), axis=1, keepdims=True)


def member_of(place, k):
    core = place[2] if k < Z else 1 - place[2]
    return k % Z * CORES + core


def hits(place, positive, k):
    rows = lax.broadcasted_iota(jnp.int32, (OWN, ROWS), 0)
    return rows == positive - (place[0] * SLAB + member_of(place, k) * OWN)


def score_body(place, users, packed, positive, items, scores, sent, share, target):
    priors = []
    for k in range(MEMBERS):
        first = pl.multiple_of(member_of(place, k) * PACK, 8)
        items[OWN * k:OWN * (k + 1), :] = packed[pl.ds(first, OWN), :]
        priors.append(column_of(packed[pl.ds(first + OWN, 8), :][0:1, 0:OWN]))
    raw = dot(items[...], users[...], 1, 1)
    wanted = positive[...]
    highest = None
    picked = jnp.zeros((OWN, ROWS), jnp.float32)
    for k in range(MEMBERS):
        at = slice(OWN * k, OWN * (k + 1))
        block = raw[at, :] - priors[k]
        scores[at, :] = block
        top = jnp.max(block, axis=0, keepdims=True)
        highest = top if k == 0 else jnp.maximum(highest, top)
        hit = hits(place, wanted, k)
        picked = picked + jnp.where(hit, block, 0.0)
        target[at, :] = jnp.where(hit, 1.0, 0.0).astype(jnp.bfloat16)
    total = jnp.sum(jnp.exp(scores[...] - highest), axis=0, keepdims=True)
    level = highest + jnp.log(total)
    picked = jnp.sum(picked, axis=0, keepdims=True)
    share[...] = jnp.exp(scores[...] - level)
    weighted = dot(share[...], items[...], 0, 0)
    rest, chosen = items[...], None
    for term in range(3):
        piece = rest.astype(jnp.bfloat16)
        rest = rest - piece.astype(jnp.float32)
        product = lax.dot_general(
            target[...], piece, (((0,), (0,)), ((), ())), preferred_element_type=jnp.float32
        )
        chosen = product if term == 0 else chosen + product
    for d in range(GROUPS):
        rows = slice(SHARE * d, SHARE * (d + 1))
        for part, value in enumerate((weighted, chosen)):
            for half in range(2):
                at = (2 * part + half) * SHARE
                sent[d, at:at + SHARE, :] = value[rows, 128 * half:128 * (half + 1)]
        for k in range(4):
            lanes = slice(128 * k, 128 * (k + 1))
            sent[d, 4 * SHARE + k:4 * SHARE + k + 1, :] = level[:, lanes]
            sent[d, 4 * SHARE + 4 + k:4 * SHARE + 5 + k, :] = picked[:, lanes]


def combine_body(place, got, loss, level, out, own):
    low = slice(4 * SHARE, 4 * SHARE + 4)
    highest = got[0, low, :]
    for d in range(1, GROUPS):
        highest = jnp.maximum(highest, got[d, low, :])
    total = jnp.zeros((4, 128), jnp.float32)
    picked = jnp.zeros((4, 128), jnp.float32)
    for d in range(GROUPS):
        total = total + jnp.exp(got[d, low, :] - highest)
        picked = picked + got[d, 4 * SHARE + 4:SENT, :]
    log_total = highest + jnp.log(total)
    loss[...] = log_total - picked
    level[...] = log_total
    row = place[0] * SHARE // 128
    lane = lax.rem(place[0] * SHARE, 128)
    here = lax.broadcasted_iota(jnp.int32, (SHARE, 128), 1) == (
        lax.broadcasted_iota(jnp.int32, (SHARE, 128), 0) + lane
    )
    own[0:4, :] = log_total
    base = own[pl.ds(row, 1), :]
    left = jnp.zeros((SHARE, 128), jnp.float32)
    right = jnp.zeros((SHARE, 128), jnp.float32)
    for d in range(GROUPS):
        part = jnp.exp(got[d, pl.ds(4 * SHARE + row, 1), :] - base)
        part = jnp.sum(jnp.where(here, part, 0.0), axis=1, keepdims=True)
        left = left + (part * got[d, 0:SHARE, :] - got[d, 2 * SHARE:3 * SHARE, :])
        right = right + (part * got[d, SHARE:2 * SHARE, :] - got[d, 3 * SHARE:4 * SHARE, :])
    for d in range(GROUPS):
        out[d, :, 0:128] = left
        out[d, :, 128:256] = right


def item_body(place, users, positive, scores, level, mine, theirs, grad):
    level = jnp.concatenate([level[k:k + 1, :] for k in range(4)], axis=1)
    wanted = positive[...]
    for k in range(MEMBERS):
        at = slice(OWN * k, OWN * (k + 1))
        hit = hits(place, wanted, k)
        grad[at, :] = jnp.exp(scores[at, :] - level) - jnp.where(hit, 1.0, 0.0)
    theirs[...] = dot(grad[HALF:SLAB, :], users[...], 1, 0)
    mine[...] = dot(grad[0:HALF, :], users[...], 1, 0)


def halve_body(shift, place, a, b, keep, send, both):
    both[...] = a[...] + b[...]
    bit = lax.rem(lax.shift_right_logical(place[1], shift), 2)
    for k in range(keep.shape[0] // OWN):
        at = slice(OWN * k, OWN * (k + 1))
        keep[at, :] = both[pl.ds(pl.multiple_of((2 * k + bit) * OWN, OWN), OWN), :]
        send[at, :] = both[pl.ds(pl.multiple_of((2 * k + 1 - bit) * OWN, OWN), OWN), :]


def sum_body(a, b, out):
    out[...] = a[...] + b[...]


def exchange(value, axis):
    return lax.all_to_all(value, axis, split_axis=0, concat_axis=0, tiled=True)


def swap(value, flip_z, flip_core):
    pairs = [
        (z * CORES + c, (z ^ flip_z) * CORES + (c ^ flip_core))
        for z in range(Z)
        for c in range(CORES)
    ]
    return lax.ppermute(value, "users", pairs)


def per_device(user_vectors, item_vectors, item_counts, positive_ids):
    member = lax.axis_index("users")
    place = jnp.stack([lax.axis_index("items"), member // CORES, member % CORES]).astype(jnp.int32)
    positive = positive_ids.reshape(1, ROWS)
    product = 2 * ROWS * SLAB * E

    packed = call(pack_body, f32(PACK, E), (item_vectors, item_counts.reshape(1, OWN)))
    packed = lax.all_gather(packed, "users", axis=0, tiled=True)
    items, scores, sent = call(
        score_body, (f32(SLAB, E), f32(SLAB, ROWS), f32(GROUPS, SENT, 128)),
        (place, user_vectors, packed, positive), scalars=1, flops=3 * product,
        scratch=[pltpu.VMEM((SLAB, ROWS), jnp.float32), pltpu.VMEM((SLAB, ROWS), jnp.bfloat16)],
    )
    got = exchange(sent, "items")
    loss, level, spread = call(
        combine_body, (f32(4, 128), f32(4, 128), f32(GROUPS, SHARE, E)), (place, got),
        scalars=1, scratch=[pltpu.VMEM((8, 128), jnp.float32)],
    )
    user_grad = exchange(spread, "items").reshape(ROWS, E)
    mine, theirs = call(
        item_body, (f32(HALF, E), f32(HALF, E)), (place, user_vectors, positive, scores, level),
        scalars=1, scratch=[pltpu.VMEM((SLAB, ROWS), jnp.float32)], flops=product,
    )
    arrived = swap(theirs, 0, 1)
    for shift in range(3):
        size = HALF >> (shift + 1)
        mine, theirs = call(
            functools.partial(halve_body, shift), (f32(size, E), f32(size, E)),
            (place, mine, arrived), scalars=1, scratch=[pltpu.VMEM((2 * size, E), jnp.float32)],
        )
        arrived = swap(theirs, 1 << shift, 0)
    item_grad = call(sum_body, f32(OWN, E), (mine, arrived))
    return (loss.reshape(ROWS), user_grad, item_grad)


def solution(mesh):
    placed = (P("users", None), P(("items", "users"), None), P(("items", "users")), P("users"))
    return jax.shard_map(
        per_device,
        mesh=mesh,
        in_specs=placed,
        out_specs=(P("users"), P("users", None), P(("items", "users"), None)),
        check_vma=False,
    )
```

```python
import functools

import jax
import jax.numpy as jnp
from jax import lax
from jax.experimental import pallas as pl
from jax.experimental.pallas import tpu as pltpu
from jax.sharding import PartitionSpec as P

HIGH = lax.Precision.HIGHEST
GROUPS, MEMBERS = 32, 16
Z, CORES = 8, 2
E = 256
OWN = 32
PACK = OWN + 8
SLAB = MEMBERS * OWN
HALF = SLAB // CORES
ROWS = 512
SHARE = ROWS // GROUPS
VMEM_LIMIT = 48 * 1024 * 1024


def vmem():
    return pl.BlockSpec(memory_space=pltpu.VMEM)


def smem():
    return pl.BlockSpec(memory_space=pltpu.SMEM)


def f32(*shape):
    return jax.ShapeDtypeStruct(shape, jnp.float32)


def call(body, out_shape, operands, scalars=0, scratch=(), flops=0, after=()):
    single = not isinstance(out_shape, (tuple, list))
    outs = [out_shape] if single else list(out_shape)
    size = sum(o.size * 4 for o in operands) + sum(4 * s.size for s in outs)
    last = len(operands)
    result = pl.pallas_call(
        (lambda *refs: body(*refs[:last], *refs[last + len(after):])) if after else body,
        out_shape=outs,
        in_specs=[smem()] * scalars + [vmem()] * (len(operands) - scalars)
        + [pl.BlockSpec(memory_space=pl.ANY)] * len(after),
        out_specs=[vmem()] * len(outs),
        scratch_shapes=list(scratch),
        compiler_params=pltpu.CompilerParams(vmem_limit_bytes=VMEM_LIMIT),
        cost_estimate=pl.CostEstimate(flops=flops, bytes_accessed=size, transcendentals=0),
    )(*operands, *after)
    return result[0] if single else result


def dot(a, b, contract_a, contract_b):
    return lax.dot_general(
        a, b, (((contract_a,), (contract_b,)), ((), ())),
        precision=HIGH, preferred_element_type=jnp.float32,
    )


def pack_body(items, counts, out):
    out[0:OWN, :] = items[...]
    priors = jnp.log(1.0 + counts[...].astype(jnp.float32))
    out[OWN:PACK, :] = jnp.zeros((PACK - OWN, E), jnp.float32)
    out[OWN:OWN + 1, 0:OWN] = priors


def column_of(row):
    size = row.shape[1]
    eye = lax.broadcasted_iota(jnp.int32, (size, size), 0) == lax.broadcasted_iota(
        jnp.int32, (size, size), 1
    )
    return jnp.sum(jnp.where(eye, jnp.broadcast_to(row, (size, size)), 0.0), axis=1, keepdims=True)


def member_of(place, k):
    core = place[2] if k < Z else 1 - place[2]
    return k % Z * CORES + core


def hits(place, positive, k):
    rows = lax.broadcasted_iota(jnp.int32, (OWN, ROWS), 0)
    return rows == positive - (place[0] * SLAB + member_of(place, k) * OWN)


def score_body(place, users, packed, positive, items, scores, stats):
    priors = []
    for k in range(MEMBERS):
        first = pl.multiple_of(member_of(place, k) * PACK, 8)
        items[OWN * k:OWN * (k + 1), :] = packed[pl.ds(first, OWN), :]
        priors.append(column_of(packed[pl.ds(first + OWN, 8), :][0:1, 0:OWN]))
    raw = dot(items[...], users[...], 1, 1)
    wanted = positive[...]
    highest = None
    picked = jnp.zeros((OWN, ROWS), jnp.float32)
    for k in range(MEMBERS):
        at = slice(OWN * k, OWN * (k + 1))
        block = raw[at, :] - priors[k]
        scores[at, :] = block
        top = jnp.max(block, axis=0, keepdims=True)
        highest = top if k == 0 else jnp.maximum(highest, top)
        picked = picked + jnp.where(hits(place, wanted, k), block, 0.0)
    total = jnp.sum(jnp.exp(scores[...] - highest), axis=0, keepdims=True)
    level = highest + jnp.log(total)
    picked = jnp.sum(picked, axis=0, keepdims=True)
    for k in range(4):
        lanes = slice(128 * k, 128 * (k + 1))
        stats[0, k:k + 1, :] = level[:, lanes]
        stats[0, 4 + k:5 + k, :] = picked[:, lanes]
    one = stats[0, :, :]
    for d in range(1, GROUPS):
        stats[d, :, :] = one


def user_body(place, items, positive, scores, stats, loss, grad, user_part):
    highest = stats[0, 0:4, :]
    for d in range(1, GROUPS):
        highest = jnp.maximum(highest, stats[d, 0:4, :])
    total = jnp.zeros((4, 128), jnp.float32)
    picked = jnp.zeros((4, 128), jnp.float32)
    for d in range(GROUPS):
        total = total + jnp.exp(stats[d, 0:4, :] - highest)
        picked = picked + stats[d, 4:8, :]
    log_total = highest + jnp.log(total)
    loss[...] = log_total - picked
    level = jnp.concatenate([log_total[k:k + 1, :] for k in range(4)], axis=1)
    wanted = positive[...]
    for k in range(MEMBERS):
        at = slice(OWN * k, OWN * (k + 1))
        hit = hits(place, wanted, k)
        grad[at, :] = jnp.exp(scores[at, :] - level) - jnp.where(hit, 1.0, 0.0)
    user_part[...] = dot(grad[...], items[...], 0, 0)


def item_body(users, grad, mine, theirs):
    theirs[...] = dot(grad[HALF:SLAB, :], users[...], 1, 0)
    mine[...] = dot(grad[0:HALF, :], users[...], 1, 0)


def add_spread_body(parts, out):
    total = parts[0]
    for r in range(1, parts.shape[0]):
        total = total + parts[r]
    for r in range(out.shape[0]):
        out[r] = total


def halve_body(shift, place, a, b, keep, send, both):
    both[...] = a[...] + b[...]
    bit = lax.rem(lax.shift_right_logical(place[1], shift), 2)
    for k in range(keep.shape[0] // OWN):
        at = slice(OWN * k, OWN * (k + 1))
        keep[at, :] = both[pl.ds(pl.multiple_of((2 * k + bit) * OWN, OWN), OWN), :]
        send[at, :] = both[pl.ds(pl.multiple_of((2 * k + 1 - bit) * OWN, OWN), OWN), :]


def sum_body(a, b, out):
    out[...] = a[...] + b[...]


def exchange(value, axis):
    return lax.all_to_all(value, axis, split_axis=0, concat_axis=0, tiled=True)


def swap(value, flip_z, flip_core):
    pairs = [
        (z * CORES + c, (z ^ flip_z) * CORES + (c ^ flip_core))
        for z in range(Z)
        for c in range(CORES)
    ]
    return lax.ppermute(value, "users", pairs)


def per_device(user_vectors, item_vectors, item_counts, positive_ids):
    member = lax.axis_index("users")
    place = jnp.stack([lax.axis_index("items"), member // CORES, member % CORES]).astype(jnp.int32)
    positive = positive_ids.reshape(1, ROWS)
    product = 2 * ROWS * SLAB * E

    packed = call(pack_body, f32(PACK, E), (item_vectors, item_counts.reshape(1, OWN)))
    packed = lax.all_gather(packed, "users", axis=0, tiled=True)
    items, scores, stats = call(
        score_body, (f32(SLAB, E), f32(SLAB, ROWS), f32(GROUPS, 8, 128)),
        (place, user_vectors, packed, positive), scalars=1, flops=product,
    )
    stats = exchange(stats, "items")
    loss, grad, user_part = call(
        user_body, (f32(4, 128), f32(SLAB, ROWS), f32(ROWS, E)),
        (place, items, positive, scores, stats), scalars=1, flops=product,
    )
    parts = exchange(user_part.reshape(GROUPS, SHARE, E), "items")
    mine, theirs = call(item_body, (f32(HALF, E), f32(HALF, E)), (user_vectors, grad), flops=product)
    arrived = swap(theirs, 0, 1)
    for shift in range(3):
        size = HALF >> (shift + 1)
        mine, theirs = call(
            functools.partial(halve_body, shift), (f32(size, E), f32(size, E)),
            (place, mine, arrived), scalars=1, scratch=[pltpu.VMEM((2 * size, E), jnp.float32)],
        )
        arrived = swap(theirs, 1 << shift, 0)
        if shift == 0:
            spread = call(add_spread_body, f32(GROUPS, SHARE, E), (parts,), after=(arrived,))
            user_grad = exchange(spread, "items").reshape(ROWS, E)
    item_grad = call(sum_body, f32(OWN, E), (mine, arrived))
    return (loss.reshape(ROWS), user_grad, item_grad)


def solution(mesh):
    placed = (P("users", None), P(("items", "users"), None), P(("items", "users")), P("users"))
    return jax.shard_map(
        per_device,
        mesh=mesh,
        in_specs=placed,
        out_specs=(P("users"), P("users", None), P(("items", "users"), None)),
        check_vma=False,
    )
```

```python
import functools

import jax
import jax.numpy as jnp
from jax import lax
from jax.experimental import pallas as pl
from jax.experimental.pallas import tpu as pltpu
from jax.sharding import PartitionSpec as P

HIGH = lax.Precision.HIGHEST
GROUPS, MEMBERS = 32, 16
Z, CORES = 8, 2
E = 256
OWN = 32
PACK = OWN + 8
SLAB = MEMBERS * OWN
HALF = SLAB // CORES
ROWS = 512
SHARE = ROWS // GROUPS
VMEM_LIMIT = 48 * 1024 * 1024


def vmem():
    return pl.BlockSpec(memory_space=pltpu.VMEM)


def smem():
    return pl.BlockSpec(memory_space=pltpu.SMEM)


def f32(*shape):
    return jax.ShapeDtypeStruct(shape, jnp.float32)


def call(body, out_shape, operands, scalars=0, scratch=(), flops=0, after=()):
    single = not isinstance(out_shape, (tuple, list))
    outs = [out_shape] if single else list(out_shape)
    size = sum(o.size * 4 for o in operands) + sum(4 * s.size for s in outs)
    last = len(operands)
    result = pl.pallas_call(
        (lambda *refs: body(*refs[:last], *refs[last + len(after):])) if after else body,
        out_shape=outs,
        in_specs=[smem()] * scalars + [vmem()] * (len(operands) - scalars)
        + [pl.BlockSpec(memory_space=pl.ANY)] * len(after),
        out_specs=[vmem()] * len(outs),
        scratch_shapes=list(scratch),
        compiler_params=pltpu.CompilerParams(vmem_limit_bytes=VMEM_LIMIT),
        cost_estimate=pl.CostEstimate(flops=flops, bytes_accessed=size, transcendentals=0),
    )(*operands, *after)
    return result[0] if single else result


def dot(a, b, contract_a, contract_b):
    return lax.dot_general(
        a, b, (((contract_a,), (contract_b,)), ((), ())),
        precision=HIGH, preferred_element_type=jnp.float32,
    )


def pack_body(items, counts, out):
    out[0:OWN, :] = items[...]
    priors = jnp.log(1.0 + counts[...].astype(jnp.float32))
    out[OWN:PACK, :] = jnp.zeros((PACK - OWN, E), jnp.float32)
    out[OWN:OWN + 1, 0:OWN] = priors


def column_of(row):
    size = row.shape[1]
    eye = lax.broadcasted_iota(jnp.int32, (size, size), 0) == lax.broadcasted_iota(
        jnp.int32, (size, size), 1
    )
    return jnp.sum(jnp.where(eye, jnp.broadcast_to(row, (size, size)), 0.0), axis=1, keepdims=True)


def member_of(place, k):
    core = place[2] if k < Z else 1 - place[2]
    return k % Z * CORES + core


def hits(place, positive, k):
    rows = lax.broadcasted_iota(jnp.int32, (OWN, ROWS), 0)
    return rows == positive - (place[0] * SLAB + member_of(place, k) * OWN)


def score_body(place, users, packed, positive, items, scores, stats):
    priors = []
    for k in range(MEMBERS):
        first = pl.multiple_of(member_of(place, k) * PACK, 8)
        items[OWN * k:OWN * (k + 1), :] = packed[pl.ds(first, OWN), :]
        priors.append(column_of(packed[pl.ds(first + OWN, 8), :][0:1, 0:OWN]))
    raw = dot(items[...], users[...], 1, 1)
    wanted = positive[...]
    highest = None
    picked = jnp.zeros((OWN, ROWS), jnp.float32)
    for k in range(MEMBERS):
        at = slice(OWN * k, OWN * (k + 1))
        block = raw[at, :] - priors[k]
        scores[at, :] = block
        top = jnp.max(block, axis=0, keepdims=True)
        highest = top if k == 0 else jnp.maximum(highest, top)
        picked = picked + jnp.where(hits(place, wanted, k), block, 0.0)
    total = jnp.sum(jnp.exp(scores[...] - highest), axis=0, keepdims=True)
    level = highest + jnp.log(total)
    picked = jnp.sum(picked, axis=0, keepdims=True)
    for k in range(4):
        lanes = slice(128 * k, 128 * (k + 1))
        stats[0, k:k + 1, :] = level[:, lanes]
        stats[0, 4 + k:5 + k, :] = picked[:, lanes]
    one = stats[0, :, :]
    for d in range(1, GROUPS):
        stats[d, :, :] = one


def weigh_body(place, items, positive, scores, stats, share, weighted, chosen, target):
    level = jnp.concatenate([stats[0, k:k + 1, :] for k in range(4)], axis=1)
    wanted = positive[...]
    for k in range(MEMBERS):
        at = slice(OWN * k, OWN * (k + 1))
        share[at, :] = jnp.exp(scores[at, :] - level)
        target[at, :] = jnp.where(hits(place, wanted, k), 1.0, 0.0).astype(jnp.bfloat16)
    weighted[...] = dot(share[...], items[...], 0, 0)
    rest = items[...]
    for term in range(3):
        piece = rest.astype(jnp.bfloat16)
        rest = rest - piece.astype(jnp.float32)
        product = lax.dot_general(
            target[...], piece, (((0,), (0,)), ((), ())), preferred_element_type=jnp.float32
        )
        chosen[...] = product if term == 0 else chosen[...] + product


def user_body(own, stats, weighted, chosen, loss, factor, user_part):
    highest = stats[0, 0:4, :]
    for d in range(1, GROUPS):
        highest = jnp.maximum(highest, stats[d, 0:4, :])
    total = jnp.zeros((4, 128), jnp.float32)
    picked = jnp.zeros((4, 128), jnp.float32)
    for d in range(GROUPS):
        total = total + jnp.exp(stats[d, 0:4, :] - highest)
        picked = picked + stats[d, 4:8, :]
    log_total = highest + jnp.log(total)
    loss[...] = log_total - picked
    factor[...] = jnp.exp(own[0, 0:4, :] - log_total)
    for k in range(4):
        at = slice(128 * k, 128 * (k + 1))
        user_part[at, :] = column_of(factor[k:k + 1, :]) * weighted[at, :] - chosen[at, :]


def item_body(place, users, positive, share, factor, mine, theirs, grad):
    scale = jnp.concatenate([factor[k:k + 1, :] for k in range(4)], axis=1)
    wanted = positive[...]
    for k in list(range(Z, MEMBERS)) + list(range(Z)):
        at = slice(OWN * k, OWN * (k + 1))
        hit = jnp.where(hits(place, wanted, k), 1.0, 0.0)
        grad[at, :] = share[at, :] * scale - hit
    theirs[...] = dot(grad[HALF:SLAB, :], users[...], 1, 0)
    mine[...] = dot(grad[0:HALF, :], users[...], 1, 0)


def add_spread_body(parts, out):
    total = parts[0]
    for r in range(1, parts.shape[0]):
        total = total + parts[r]
    for r in range(out.shape[0]):
        out[r] = total


def halve_body(shift, place, a, b, keep, send, both):
    both[...] = a[...] + b[...]
    bit = lax.rem(lax.shift_right_logical(place[1], shift), 2)
    for k in range(keep.shape[0] // OWN):
        at = slice(OWN * k, OWN * (k + 1))
        keep[at, :] = both[pl.ds(pl.multiple_of((2 * k + bit) * OWN, OWN), OWN), :]
        send[at, :] = both[pl.ds(pl.multiple_of((2 * k + 1 - bit) * OWN, OWN), OWN), :]


def sum_body(a, b, out):
    out[...] = a[...] + b[...]


def exchange(value, axis):
    return lax.all_to_all(value, axis, split_axis=0, concat_axis=0, tiled=True)


def swap(value, flip_z, flip_core):
    pairs = [
        (z * CORES + c, (z ^ flip_z) * CORES + (c ^ flip_core))
        for z in range(Z)
        for c in range(CORES)
    ]
    return lax.ppermute(value, "users", pairs)


def per_device(user_vectors, item_vectors, item_counts, positive_ids):
    member = lax.axis_index("users")
    place = jnp.stack([lax.axis_index("items"), member // CORES, member % CORES]).astype(jnp.int32)
    product = 2 * ROWS * SLAB * E
    users, positive = user_vectors, positive_ids.reshape(1, ROWS)
    packed = call(pack_body, f32(PACK, E), (item_vectors, item_counts.reshape(1, OWN)))
    packed = lax.all_gather(packed, "users", axis=0, tiled=True)
    items, scores, own = call(
        score_body, (f32(SLAB, E), f32(SLAB, ROWS), f32(GROUPS, 8, 128)),
        (place, users, packed, positive), scalars=1, flops=product,
    )
    stats = exchange(own, "items")
    share, weighted, chosen = call(
        weigh_body, (f32(SLAB, ROWS), f32(ROWS, E), f32(ROWS, E)),
        (place, items, positive, scores, own), scalars=1, flops=2 * product,
        scratch=[pltpu.VMEM((SLAB, ROWS), jnp.bfloat16)],
    )
    loss, factor, user_part = call(
        user_body, (f32(4, 128), f32(4, 128), f32(ROWS, E)), (own, stats, weighted, chosen),
    )
    parts = exchange(user_part.reshape(GROUPS, SHARE, E), "items")
    mine, theirs = call(
        item_body, (f32(HALF, E), f32(HALF, E)), (place, users, positive, share, factor),
        scalars=1, flops=product, scratch=[pltpu.VMEM((SLAB, ROWS), jnp.float32)],
    )
    arrived = swap(theirs, 0, 1)
    for shift in range(3):
        size = HALF >> (shift + 1)
        mine, theirs = call(
            functools.partial(halve_body, shift), (f32(size, E), f32(size, E)),
            (place, mine, arrived), scalars=1, scratch=[pltpu.VMEM((2 * size, E), jnp.float32)],
        )
        if shift == 1:
            spread = call(add_spread_body, f32(GROUPS, SHARE, E), (parts,), after=(theirs,))
            user_grad = exchange(spread, "items").reshape(ROWS, E)
        arrived = swap(theirs, 1 << shift, 0)
    item_grad = call(sum_body, f32(OWN, E), (mine, arrived))
    return (loss.reshape(ROWS), user_grad, item_grad)


def solution(mesh):
    placed = (P("users", None), P(("items", "users"), None), P(("items", "users")), P("users"))
    return jax.shard_map(
        per_device,
        mesh=mesh,
        in_specs=placed,
        out_specs=(P("users"), P("users", None), P(("items", "users"), None)),
        check_vma=False,
    )
```

```python
import jax
import jax.numpy as jnp
from jax import lax
from jax.experimental import pallas as pl
from jax.experimental.pallas import tpu as pltpu
from jax.sharding import PartitionSpec as P

HIGH = lax.Precision.HIGHEST
GROUPS, MEMBERS = 32, 16
Z, CORES = 8, 2
E = 256
OWN = 32
PACK = OWN + 8
SLAB = MEMBERS * OWN
HALF = SLAB // CORES
ROWS = 512
SHARE = ROWS // GROUPS
VMEM_LIMIT = 48 * 1024 * 1024


def vmem():
    return pl.BlockSpec(memory_space=pltpu.VMEM)


def smem():
    return pl.BlockSpec(memory_space=pltpu.SMEM)


def f32(*shape):
    return jax.ShapeDtypeStruct(shape, jnp.float32)


def call(body, out_shape, operands, scalars=0, scratch=(), flops=0, after=()):
    single = not isinstance(out_shape, (tuple, list))
    outs = [out_shape] if single else list(out_shape)
    size = sum(o.size * 4 for o in operands) + sum(4 * s.size for s in outs)
    last = len(operands)
    result = pl.pallas_call(
        (lambda *refs: body(*refs[:last], *refs[last + len(after):])) if after else body,
        out_shape=outs,
        in_specs=[smem()] * scalars + [vmem()] * (len(operands) - scalars)
        + [pl.BlockSpec(memory_space=pl.ANY)] * len(after),
        out_specs=[vmem()] * len(outs),
        scratch_shapes=list(scratch),
        compiler_params=pltpu.CompilerParams(vmem_limit_bytes=VMEM_LIMIT),
        cost_estimate=pl.CostEstimate(flops=flops, bytes_accessed=size, transcendentals=0),
    )(*operands, *after)
    return result[0] if single else result


def dot(a, b, contract_a, contract_b):
    return lax.dot_general(
        a, b, (((contract_a,), (contract_b,)), ((), ())),
        precision=HIGH, preferred_element_type=jnp.float32,
    )


def split(a):
    high = a.astype(jnp.bfloat16)
    return high, (a - high.astype(jnp.float32)).astype(jnp.bfloat16)


def dot_split(a, b, contract_a, contract_b):
    (a_high, a_low), (b_high, b_low) = a, b

    def product(left, right):
        return lax.dot_general(
            left, right, (((contract_a,), (contract_b,)), ((), ())),
            preferred_element_type=jnp.float32,
        )

    return product(a_high, b_high) + (product(a_high, b_low) + product(a_low, b_high))


def pack_body(items, counts, out):
    out[0:OWN, :] = items[...]
    priors = jnp.log(1.0 + counts[...].astype(jnp.float32))
    out[OWN:PACK, :] = jnp.zeros((PACK - OWN, E), jnp.float32)
    out[OWN:OWN + 1, 0:OWN] = priors


def column_of(row):
    size = row.shape[1]
    eye = lax.broadcasted_iota(jnp.int32, (size, size), 0) == lax.broadcasted_iota(
        jnp.int32, (size, size), 1
    )
    return jnp.sum(jnp.where(eye, jnp.broadcast_to(row, (size, size)), 0.0), axis=1, keepdims=True)


def member_of(place, k):
    core = place[2] if k < Z else 1 - place[2]
    return k % Z * CORES + core


def hits(place, positive, k):
    rows = lax.broadcasted_iota(jnp.int32, (OWN, ROWS), 0)
    return rows == positive - (place[0] * SLAB + member_of(place, k) * OWN)


def score_body(place, users, packed, positive, items, scores, stats):
    priors = []
    for k in range(MEMBERS):
        first = pl.multiple_of(member_of(place, k) * PACK, 8)
        items[OWN * k:OWN * (k + 1), :] = packed[pl.ds(first, OWN), :]
        priors.append(column_of(packed[pl.ds(first + OWN, 8), :][0:1, 0:OWN]))
    raw = dot(items[...], users[...], 1, 1)
    wanted = positive[...]
    highest = None
    picked = jnp.zeros((OWN, ROWS), jnp.float32)
    for k in range(MEMBERS):
        at = slice(OWN * k, OWN * (k + 1))
        block = raw[at, :] - priors[k]
        scores[at, :] = block
        top = jnp.max(block, axis=0, keepdims=True)
        highest = top if k == 0 else jnp.maximum(highest, top)
        picked = picked + jnp.where(hits(place, wanted, k), block, 0.0)
    total = jnp.sum(jnp.exp(scores[...] - highest), axis=0, keepdims=True)
    level = highest + jnp.log(total)
    picked = jnp.sum(picked, axis=0, keepdims=True)
    for k in range(4):
        lanes = slice(128 * k, 128 * (k + 1))
        stats[0, k:k + 1, :] = level[:, lanes]
        stats[0, 4 + k:5 + k, :] = picked[:, lanes]
    one = stats[0, :, :]
    for d in range(1, GROUPS):
        stats[d, :, :] = one


def user_body(place, items, positive, scores, stats, loss, grad, user_part):
    highest = stats[0, 0:4, :]
    for d in range(1, GROUPS):
        highest = jnp.maximum(highest, stats[d, 0:4, :])
    total = jnp.zeros((4, 128), jnp.float32)
    picked = jnp.zeros((4, 128), jnp.float32)
    for d in range(GROUPS):
        total = total + jnp.exp(stats[d, 0:4, :] - highest)
        picked = picked + stats[d, 4:8, :]
    log_total = highest + jnp.log(total)
    loss[...] = log_total - picked
    level = jnp.concatenate([log_total[k:k + 1, :] for k in range(4)], axis=1)
    wanted = positive[...]
    for k in range(MEMBERS):
        at = slice(OWN * k, OWN * (k + 1))
        hit = hits(place, wanted, k)
        grad[at, :] = jnp.exp(scores[at, :] - level) - jnp.where(hit, 1.0, 0.0)
    user_part[...] = dot_split(split(grad[...]), split(items[...]), 0, 0)


def item_body(users, grad, mine, theirs):
    right = split(users[...])
    theirs[...] = dot_split(split(grad[HALF:SLAB, :]), right, 1, 0)
    mine[...] = dot_split(split(grad[0:HALF, :]), right, 1, 0)


def add_spread_body(parts, out):
    total = parts[0]
    for r in range(1, parts.shape[0]):
        total = total + parts[r]
    for r in range(out.shape[0]):
        out[r] = total


def halve_body(place, a, b, keep, send, both):
    both[...] = a[...] + b[...]
    bit = lax.rem(place[1], 2)
    for k in range(keep.shape[0] // OWN):
        at = slice(OWN * k, OWN * (k + 1))
        keep[at, :] = both[pl.ds(pl.multiple_of((2 * k + bit) * OWN, OWN), OWN), :]
        send[at, :] = both[pl.ds(pl.multiple_of((2 * k + 1 - bit) * OWN, OWN), OWN), :]


def deal_body(place, a, b, *outs):
    *outs, both = outs
    both[...] = a[...] + b[...]
    for r, out in enumerate(outs):
        pair = lax.rem(lax.shift_right_logical(place[1], 1) + r, Z // 2)
        out[...] = both[pl.ds(pl.multiple_of(pair * OWN, OWN), OWN), :]


def sum_body(*refs):
    total = refs[0][...]
    for ref in refs[1:-1]:
        total = total + ref[...]
    refs[-1][...] = total


def exchange(value, axis):
    return lax.all_to_all(value, axis, split_axis=0, concat_axis=0, tiled=True)


def move(value, target):
    pairs = []
    for z in range(Z):
        for c in range(CORES):
            z_to, c_to = target(z, c)
            pairs.append((z * CORES + c, z_to % Z * CORES + c_to))
    return lax.ppermute(value, "users", pairs)


def per_device(user_vectors, item_vectors, item_counts, positive_ids):
    member = lax.axis_index("users")
    place = jnp.stack([lax.axis_index("items"), member // CORES, member % CORES]).astype(jnp.int32)
    positive = positive_ids.reshape(1, ROWS)
    product = 2 * ROWS * SLAB * E

    packed = call(pack_body, f32(PACK, E), (item_vectors, item_counts.reshape(1, OWN)))
    packed = lax.all_gather(packed, "users", axis=0, tiled=True)
    items, scores, stats = call(
        score_body, (f32(SLAB, E), f32(SLAB, ROWS), f32(GROUPS, 8, 128)),
        (place, user_vectors, packed, positive), scalars=1, flops=product,
    )
    stats = exchange(stats, "items")
    loss, grad, user_part = call(
        user_body, (f32(4, 128), f32(SLAB, ROWS), f32(ROWS, E)),
        (place, items, positive, scores, stats), scalars=1, flops=product,
    )
    parts = exchange(user_part.reshape(GROUPS, SHARE, E), "items")
    mine, theirs = call(item_body, (f32(HALF, E), f32(HALF, E)), (user_vectors, grad), flops=product)
    arrived = move(theirs, lambda z, c: (z, 1 - c))
    mine, theirs = call(
        halve_body, [f32(HALF // 2, E)] * 2, (place, mine, arrived), scalars=1,
        scratch=[pltpu.VMEM((HALF, E), jnp.float32)],
    )
    arrived = move(theirs, lambda z, c: (z ^ 1, c))
    pieces = call(
        deal_body, [f32(OWN, E)] * (Z // 2), (place, mine, arrived), scalars=1,
        scratch=[pltpu.VMEM((HALF // 2, E), jnp.float32)],
    )
    spread = call(add_spread_body, f32(GROUPS, SHARE, E), (parts,), after=(pieces[0],))
    user_grad = exchange(spread, "items").reshape(ROWS, E)
    terms = [pieces[0]]
    for r in (2, 1, 3):
        terms.append(move(pieces[r], lambda z, c, r=r: (z + 2 * r, c)))
    item_grad = call(sum_body, f32(OWN, E), terms)
    return (loss.reshape(ROWS), user_grad, item_grad)


def solution(mesh):
    placed = (P("users", None), P(("items", "users"), None), P(("items", "users")), P("users"))
    return jax.shard_map(
        per_device,
        mesh=mesh,
        in_specs=placed,
        out_specs=(P("users"), P("users", None), P(("items", "users"), None)),
        check_vma=False,
    )
```

```python
import jax
import jax.numpy as jnp
from jax import lax
from jax.experimental import pallas as pl
from jax.experimental.pallas import tpu as pltpu
from jax.sharding import Mesh, PartitionSpec as P

HIGH = lax.Precision.HIGHEST
X, Y, Z, CORES = 4, 8, 8, 2
GROUPS, MEMBERS = X * Y, Z * CORES
PEERS = ("y", "x")
USER_AXES = ("z", "core")
E = 256
OWN = 32
PACK = OWN + 8
SLAB = MEMBERS * OWN
HALF = SLAB // CORES
ROWS = 512
SHARE = ROWS // GROUPS
VMEM_LIMIT = 48 * 1024 * 1024


def vmem():
    return pl.BlockSpec(memory_space=pltpu.VMEM)


def smem():
    return pl.BlockSpec(memory_space=pltpu.SMEM)


def f32(*shape):
    return jax.ShapeDtypeStruct(shape, jnp.float32)


def call(body, out_shape, operands, scalars=0, scratch=(), flops=0, after=()):
    single = not isinstance(out_shape, (tuple, list))
    outs = [out_shape] if single else list(out_shape)
    size = sum(o.size * 4 for o in operands) + sum(4 * s.size for s in outs)
    last = len(operands)
    result = pl.pallas_call(
        (lambda *refs: body(*refs[:last], *refs[last + len(after):])) if after else body,
        out_shape=outs,
        in_specs=[smem()] * scalars + [vmem()] * (len(operands) - scalars)
        + [pl.BlockSpec(memory_space=pl.ANY)] * len(after),
        out_specs=[vmem()] * len(outs),
        scratch_shapes=list(scratch),
        compiler_params=pltpu.CompilerParams(vmem_limit_bytes=VMEM_LIMIT),
        cost_estimate=pl.CostEstimate(flops=flops, bytes_accessed=size, transcendentals=0),
    )(*operands, *after)
    return result[0] if single else result


def dot(a, b, contract_a, contract_b):
    return lax.dot_general(
        a, b, (((contract_a,), (contract_b,)), ((), ())),
        precision=HIGH, preferred_element_type=jnp.float32,
    )


def split(a):
    high = a.astype(jnp.bfloat16)
    return high, (a - high.astype(jnp.float32)).astype(jnp.bfloat16)


def dot_split(a, b, contract_a, contract_b):
    (a_high, a_low), (b_high, b_low) = a, b

    def product(left, right):
        return lax.dot_general(
            left, right, (((contract_a,), (contract_b,)), ((), ())),
            preferred_element_type=jnp.float32,
        )

    return product(a_high, b_high) + (product(a_high, b_low) + product(a_low, b_high))


def pack_body(items, counts, out):
    out[0:OWN, :] = items[...]
    priors = jnp.log(1.0 + counts[...].astype(jnp.float32))
    out[OWN:PACK, :] = jnp.zeros((PACK - OWN, E), jnp.float32)
    out[OWN:OWN + 1, 0:OWN] = priors


def column_of(row):
    size = row.shape[1]
    eye = lax.broadcasted_iota(jnp.int32, (size, size), 0) == lax.broadcasted_iota(
        jnp.int32, (size, size), 1
    )
    return jnp.sum(jnp.where(eye, jnp.broadcast_to(row, (size, size)), 0.0), axis=1, keepdims=True)


def member_of(place, k):
    core = place[2] if k < Z else 1 - place[2]
    return k % Z * CORES + core


def hits(place, positive, k):
    rows = lax.broadcasted_iota(jnp.int32, (OWN, ROWS), 0)
    return rows == positive - (place[0] * SLAB + member_of(place, k) * OWN)


def score_body(place, users, packed, positive, items, scores, stats):
    priors = []
    for k in range(MEMBERS):
        first = pl.multiple_of(member_of(place, k) * PACK, 8)
        items[OWN * k:OWN * (k + 1), :] = packed[pl.ds(first, OWN), :]
        priors.append(column_of(packed[pl.ds(first + OWN, 8), :][0:1, 0:OWN]))
    raw = dot(items[...], users[...], 1, 1)
    wanted = positive[...]
    highest = None
    picked = jnp.zeros((OWN, ROWS), jnp.float32)
    for k in range(MEMBERS):
        at = slice(OWN * k, OWN * (k + 1))
        block = raw[at, :] - priors[k]
        scores[at, :] = block
        top = jnp.max(block, axis=0, keepdims=True)
        highest = top if k == 0 else jnp.maximum(highest, top)
        picked = picked + jnp.where(hits(place, wanted, k), block, 0.0)
    total = jnp.sum(jnp.exp(scores[...] - highest), axis=0, keepdims=True)
    level = highest + jnp.log(total)
    picked = jnp.sum(picked, axis=0, keepdims=True)
    for k in range(4):
        lanes = slice(128 * k, 128 * (k + 1))
        stats[0, k:k + 1, :] = level[:, lanes]
        stats[0, 4 + k:5 + k, :] = picked[:, lanes]
    one = stats[0, :, :]
    for d in range(1, GROUPS):
        stats[d, :, :] = one


def user_body(place, items, positive, scores, stats, loss, grad, user_part):
    highest = stats[0, 0:4, :]
    for d in range(1, GROUPS):
        highest = jnp.maximum(highest, stats[d, 0:4, :])
    total = jnp.zeros((4, 128), jnp.float32)
    picked = jnp.zeros((4, 128), jnp.float32)
    for d in range(GROUPS):
        total = total + jnp.exp(stats[d, 0:4, :] - highest)
        picked = picked + stats[d, 4:8, :]
    log_total = highest + jnp.log(total)
    loss[...] = log_total - picked
    level = jnp.concatenate([log_total[k:k + 1, :] for k in range(4)], axis=1)
    wanted = positive[...]
    for k in range(MEMBERS):
        at = slice(OWN * k, OWN * (k + 1))
        hit = hits(place, wanted, k)
        grad[at, :] = jnp.exp(scores[at, :] - level) - jnp.where(hit, 1.0, 0.0)
    user_part[...] = dot_split(split(grad[...]), split(items[...]), 0, 0)


def item_body(users, grad, mine, theirs):
    right = split(users[...])
    theirs[...] = dot_split(split(grad[HALF:SLAB, :]), right, 1, 0)
    mine[...] = dot_split(split(grad[0:HALF, :]), right, 1, 0)


def add_spread_body(parts, out):
    total = parts[0]
    for r in range(1, parts.shape[0]):
        total = total + parts[r]
    for r in range(out.shape[0]):
        out[r] = total


def halve_body(place, a, b, keep, send):
    bit = lax.rem(place[1], 2)
    for k in range(keep.shape[0] // OWN):
        at = slice(OWN * k, OWN * (k + 1))
        here = pl.ds(pl.multiple_of((2 * k + bit) * OWN, OWN), OWN)
        there = pl.ds(pl.multiple_of((2 * k + 1 - bit) * OWN, OWN), OWN)
        send[at, :] = a[there, :] + b[there, :]
        keep[at, :] = a[here, :] + b[here, :]


def deal_body(place, a, b, *outs):
    for r, out in enumerate(outs):
        pair = lax.rem(lax.shift_right_logical(place[1], 1) + r, Z // 2)
        rows = pl.ds(pl.multiple_of(pair * OWN, OWN), OWN)
        out[...] = a[rows, :] + b[rows, :]


def sum_body(*refs):
    total = refs[0][...]
    for ref in refs[1:-1]:
        total = total + ref[...]
    refs[-1][...] = total


def exchange(value, axis):
    return lax.all_to_all(value, axis, split_axis=0, concat_axis=0, tiled=True)


def move(value, target):
    pairs = []
    for z in range(Z):
        for c in range(CORES):
            z_to, c_to = target(z, c)
            pairs.append((z * CORES + c, z_to % Z * CORES + c_to))
    return lax.ppermute(value, USER_AXES, pairs)


def per_device(user_vectors, item_vectors, item_counts, positive_ids):
    place = jnp.stack([lax.axis_index(("x", "y")), lax.axis_index("z"), lax.axis_index("core")])
    place = place.astype(jnp.int32)
    positive = positive_ids.reshape(1, ROWS)
    product = 2 * ROWS * SLAB * E

    packed = call(pack_body, f32(PACK, E), (item_vectors, item_counts.reshape(1, OWN)))
    packed = lax.all_gather(packed, USER_AXES, axis=0, tiled=True)
    items, scores, stats = call(
        score_body, (f32(SLAB, E), f32(SLAB, ROWS), f32(GROUPS, 8, 128)),
        (place, user_vectors, packed, positive), scalars=1, flops=product,
    )
    stats = exchange(stats, PEERS)
    loss, grad, user_part = call(
        user_body, (f32(4, 128), f32(SLAB, ROWS), f32(ROWS, E)),
        (place, items, positive, scores, stats), scalars=1, flops=product,
    )
    parts = exchange(user_part.reshape(GROUPS, SHARE, E), PEERS)
    mine, theirs = call(item_body, (f32(HALF, E), f32(HALF, E)), (user_vectors, grad), flops=product)
    arrived = move(theirs, lambda z, c: (z, 1 - c))
    mine, theirs = call(
        halve_body, [f32(HALF // 2, E)] * 2, (place, mine, arrived), scalars=1,
    )
    arrived = move(theirs, lambda z, c: (z ^ 1, c))
    pieces = call(
        deal_body, [f32(OWN, E)] * (Z // 2), (place, mine, arrived), scalars=1,
    )
    spread = call(add_spread_body, f32(GROUPS, SHARE, E), (parts,), after=(pieces[0],))
    user_grad = exchange(spread, PEERS).reshape(ROWS, E)
    terms = [pieces[0]]
    for r in (2, 1, 3):
        terms.append(move(pieces[r], lambda z, c, r=r: (z + 2 * r, c)))
    item_grad = call(sum_body, f32(OWN, E), terms)
    return (loss.reshape(ROWS), user_grad, item_grad)


def solution(mesh):
    fine = Mesh(mesh.devices.reshape(X, Y, Z, CORES), ("x", "y") + USER_AXES)
    users, everything = P(USER_AXES), P(("x", "y") + USER_AXES)
    return jax.shard_map(
        per_device,
        mesh=fine,
        in_specs=(users, everything, everything, users),
        out_specs=(users, users, everything),
        check_vma=False,
    )
```

```python
import jax
import jax.numpy as jnp
from jax import lax
from jax.experimental import pallas as pl
from jax.experimental.pallas import tpu as pltpu
from jax.sharding import Mesh, PartitionSpec as P

HIGH = lax.Precision.HIGHEST
X, Y, Z, CORES = 4, 8, 8, 2
GROUPS, MEMBERS = X * Y, Z * CORES
PEERS = ("y", "x")
USER_AXES = ("z", "core")
E = 256
OWN = 32
PACK = OWN + 8
SLAB = MEMBERS * OWN
HALF = SLAB // CORES
ROWS = 512
SHARE = ROWS // GROUPS
VMEM_LIMIT = 48 * 1024 * 1024


def vmem():
    return pl.BlockSpec(memory_space=pltpu.VMEM)


def smem():
    return pl.BlockSpec(memory_space=pltpu.SMEM)


def f32(*shape):
    return jax.ShapeDtypeStruct(shape, jnp.float32)


def call(body, out_shape, operands, scalars=0, scratch=(), flops=0, after=()):
    single = not isinstance(out_shape, (tuple, list))
    outs = [out_shape] if single else list(out_shape)
    size = sum(o.size * 4 for o in operands) + sum(4 * s.size for s in outs)
    last = len(operands)
    result = pl.pallas_call(
        (lambda *refs: body(*refs[:last], *refs[last + len(after):])) if after else body,
        out_shape=outs,
        in_specs=[smem()] * scalars + [vmem()] * (len(operands) - scalars)
        + [pl.BlockSpec(memory_space=pl.ANY)] * len(after),
        out_specs=[vmem()] * len(outs),
        scratch_shapes=list(scratch),
        compiler_params=pltpu.CompilerParams(vmem_limit_bytes=VMEM_LIMIT),
        cost_estimate=pl.CostEstimate(flops=flops, bytes_accessed=size, transcendentals=0),
    )(*operands, *after)
    return result[0] if single else result


def dot(a, b, contract_a, contract_b):
    return lax.dot_general(
        a, b, (((contract_a,), (contract_b,)), ((), ())),
        precision=HIGH, preferred_element_type=jnp.float32,
    )


def split(a):
    high = a.astype(jnp.bfloat16)
    return high, (a - high.astype(jnp.float32)).astype(jnp.bfloat16)


def dot_split(a, b, contract_a, contract_b):
    (a_high, a_low), (b_high, b_low) = a, b

    def product(left, right):
        return lax.dot_general(
            left, right, (((contract_a,), (contract_b,)), ((), ())),
            preferred_element_type=jnp.float32,
        )

    return product(a_high, b_high) + (product(a_high, b_low) + product(a_low, b_high))


def pack_body(items, counts, out):
    out[0:OWN, :] = items[...]
    priors = jnp.log(1.0 + counts[...].astype(jnp.float32))
    out[OWN:PACK, :] = jnp.zeros((PACK - OWN, E), jnp.float32)
    out[OWN:OWN + 1, 0:OWN] = priors


def column_of(row):
    size = row.shape[1]
    eye = lax.broadcasted_iota(jnp.int32, (size, size), 0) == lax.broadcasted_iota(
        jnp.int32, (size, size), 1
    )
    return jnp.sum(jnp.where(eye, jnp.broadcast_to(row, (size, size)), 0.0), axis=1, keepdims=True)


def member_of(place, k):
    core = place[2] if k < Z else 1 - place[2]
    return k % Z * CORES + core


def hits(place, positive, k):
    rows = lax.broadcasted_iota(jnp.int32, (OWN, ROWS), 0)
    return rows == positive - (place[0] * SLAB + member_of(place, k) * OWN)


def score_body(place, users, packed, positive, items, scores, stats):
    priors = []
    for k in range(MEMBERS):
        first = pl.multiple_of(member_of(place, k) * PACK, 8)
        items[OWN * k:OWN * (k + 1), :] = packed[pl.ds(first, OWN), :]
        priors.append(column_of(packed[pl.ds(first + OWN, 8), :][0:1, 0:OWN]))
    raw = dot(items[...], users[...], 1, 1)
    wanted = positive[...]
    highest = None
    picked = jnp.zeros((OWN, ROWS), jnp.float32)
    for k in range(MEMBERS):
        at = slice(OWN * k, OWN * (k + 1))
        block = raw[at, :] - priors[k]
        scores[at, :] = block
        top = jnp.max(block, axis=0, keepdims=True)
        highest = top if k == 0 else jnp.maximum(highest, top)
        picked = picked + jnp.where(hits(place, wanted, k), block, 0.0)
    total = jnp.sum(jnp.exp(scores[...] - highest), axis=0, keepdims=True)
    level = highest + jnp.log(total)
    picked = jnp.sum(picked, axis=0, keepdims=True)
    for k in range(4):
        lanes = slice(128 * k, 128 * (k + 1))
        stats[0, k:k + 1, :] = level[:, lanes]
        stats[0, 4 + k:5 + k, :] = picked[:, lanes]
    one = stats[0, :, :]
    for d in range(1, GROUPS):
        stats[d, :, :] = one


def user_body(place, items, positive, scores, stats, loss, grad, user_part):
    highest = stats[0, 0:4, :]
    for d in range(1, GROUPS):
        highest = jnp.maximum(highest, stats[d, 0:4, :])
    total = jnp.zeros((4, 128), jnp.float32)
    picked = jnp.zeros((4, 128), jnp.float32)
    for d in range(GROUPS):
        total = total + jnp.exp(stats[d, 0:4, :] - highest)
        picked = picked + stats[d, 4:8, :]
    log_total = highest + jnp.log(total)
    loss[...] = log_total - picked
    level = jnp.concatenate([log_total[k:k + 1, :] for k in range(4)], axis=1)
    wanted = positive[...]
    for k in range(MEMBERS):
        at = slice(OWN * k, OWN * (k + 1))
        hit = hits(place, wanted, k)
        grad[at, :] = jnp.exp(scores[at, :] - level) - jnp.where(hit, 1.0, 0.0)
    user_part[...] = dot_split(split(grad[...]), split(items[...]), 0, 0)


def item_body(users, grad, mine, theirs):
    right = split(users[...])
    theirs[...] = dot_split(split(grad[HALF:SLAB, :]), right, 1, 0)
    mine[...] = dot_split(split(grad[0:HALF, :]), right, 1, 0)


def add_spread_body(parts, out):
    total = parts[0]
    for r in range(1, parts.shape[0]):
        total = total + parts[r]
    for r in range(out.shape[0]):
        out[r] = total


def halve_body(place, a, b, keep, send):
    bit = lax.rem(place[1], 2)
    for k in range(keep.shape[0] // OWN):
        at = slice(OWN * k, OWN * (k + 1))
        here = pl.ds(pl.multiple_of((2 * k + bit) * OWN, OWN), OWN)
        there = pl.ds(pl.multiple_of((2 * k + 1 - bit) * OWN, OWN), OWN)
        send[at, :] = a[there, :] + b[there, :]
        keep[at, :] = a[here, :] + b[here, :]


def deal_body(place, a, b, *outs):
    for r, out in enumerate(outs):
        pair = lax.rem(lax.shift_right_logical(place[1], 1) + r, Z // 2)
        rows = pl.ds(pl.multiple_of(pair * OWN, OWN), OWN)
        out[...] = a[rows, :] + b[rows, :]


def finish_body(user_rows, *refs):
    terms, (item_grad, user_grad, sent) = refs[:-3], refs[-3:]
    copy = pltpu.make_async_copy(user_rows, user_grad, sent.at[0])
    copy.start()
    total = terms[0][...]
    for ref in terms[1:]:
        total = total + ref[...]
    item_grad[...] = total
    copy.wait()


def exchange(value, axis):
    return lax.all_to_all(value, axis, split_axis=0, concat_axis=0, tiled=True)


def move(value, target):
    pairs = []
    for z in range(Z):
        for c in range(CORES):
            z_to, c_to = target(z, c)
            pairs.append((z * CORES + c, z_to % Z * CORES + c_to))
    return lax.ppermute(value, USER_AXES, pairs)


def per_device(user_vectors, item_vectors, item_counts, positive_ids):
    place = jnp.stack([lax.axis_index(("x", "y")), lax.axis_index("z"), lax.axis_index("core")])
    place = place.astype(jnp.int32)
    positive = positive_ids.reshape(1, ROWS)
    product = 2 * ROWS * SLAB * E

    packed = call(pack_body, f32(PACK, E), (item_vectors, item_counts.reshape(1, OWN)))
    packed = lax.all_gather(packed, USER_AXES, axis=0, tiled=True)
    items, scores, stats = call(
        score_body, (f32(SLAB, E), f32(SLAB, ROWS), f32(GROUPS, 8, 128)),
        (place, user_vectors, packed, positive), scalars=1, flops=product,
    )
    stats = exchange(stats, PEERS)
    loss, grad, user_part = call(
        user_body, (f32(4, 128), f32(SLAB, ROWS), f32(ROWS, E)),
        (place, items, positive, scores, stats), scalars=1, flops=product,
    )
    parts = exchange(user_part.reshape(GROUPS, SHARE, E), PEERS)
    mine, theirs = call(item_body, (f32(HALF, E), f32(HALF, E)), (user_vectors, grad), flops=product)
    arrived = move(theirs, lambda z, c: (z, 1 - c))
    mine, theirs = call(
        halve_body, [f32(HALF // 2, E)] * 2, (place, mine, arrived), scalars=1,
    )
    arrived = move(theirs, lambda z, c: (z ^ 1, c))
    pieces = call(
        deal_body, [f32(OWN, E)] * (Z // 2), (place, mine, arrived), scalars=1,
    )
    spread = call(add_spread_body, f32(GROUPS, SHARE, E), (parts,), after=(pieces[0],))
    user_rows = exchange(spread, PEERS).reshape(ROWS, E)
    terms = [pieces[0]]
    for r in (2, 1, 3):
        terms.append(move(pieces[r], lambda z, c, r=r: (z + 2 * r, c)))
    item_grad, user_grad = pl.pallas_call(
        finish_body,
        out_shape=(f32(OWN, E), f32(ROWS, E)),
        in_specs=[pl.BlockSpec(memory_space=pl.ANY)] + [vmem()] * len(terms),
        out_specs=(vmem(), pl.BlockSpec(memory_space=pl.ANY)),
        scratch_shapes=[pltpu.SemaphoreType.DMA((1,))],
        compiler_params=pltpu.CompilerParams(vmem_limit_bytes=VMEM_LIMIT),
    )(user_rows, *terms)
    return (loss.reshape(ROWS), user_grad, item_grad)


def solution(mesh):
    fine = Mesh(mesh.devices.reshape(X, Y, Z, CORES), ("x", "y") + USER_AXES)
    users, everything = P(USER_AXES), P(("x", "y") + USER_AXES)
    return jax.shard_map(
        per_device,
        mesh=fine,
        in_specs=(users, everything, everything, users),
        out_specs=(users, users, everything),
        check_vma=False,
    )
```

```python
import jax
import jax.numpy as jnp
from jax import lax
from jax.experimental import pallas as pl
from jax.experimental.pallas import tpu as pltpu
from jax.sharding import Mesh, PartitionSpec as P

HIGH = lax.Precision.HIGHEST
X, Y, Z, CORES = 4, 8, 8, 2
GROUPS, MEMBERS = X * Y, Z * CORES
PEERS = ("y", "x")
USER_AXES = ("z", "core")
E = 256
OWN = 32
PACK = OWN + 8
SLAB = MEMBERS * OWN
HALF = SLAB // CORES
ROWS = 512
SHARE = ROWS // GROUPS
VMEM_LIMIT = 48 * 1024 * 1024


def vmem():
    return pl.BlockSpec(memory_space=pltpu.VMEM)


def anywhere():
    return pl.BlockSpec(memory_space=pl.ANY)


def smem():
    return pl.BlockSpec(memory_space=pltpu.SMEM)


def f32(*shape):
    return jax.ShapeDtypeStruct(shape, jnp.float32)


def call(body, out_shape, operands, scalars=0, scratch=(), flops=0, after=(), far=()):
    single = not isinstance(out_shape, (tuple, list))
    outs = [out_shape] if single else list(out_shape)
    size = sum(o.size * 4 for o in operands) + sum(4 * s.size for s in outs)
    last = len(operands)
    result = pl.pallas_call(
        (lambda *refs: body(*refs[:last], *refs[last + len(after):])) if after else body,
        out_shape=outs,
        in_specs=[smem()] * scalars + [vmem()] * (len(operands) - scalars)
        + [anywhere()] * len(after),
        out_specs=[anywhere() if k in far else vmem() for k in range(len(outs))],
        scratch_shapes=list(scratch),
        compiler_params=pltpu.CompilerParams(vmem_limit_bytes=VMEM_LIMIT),
        cost_estimate=pl.CostEstimate(flops=flops, bytes_accessed=size, transcendentals=0),
    )(*operands, *after)
    return result[0] if single else result


def dot(a, b, contract_a, contract_b):
    return lax.dot_general(
        a, b, (((contract_a,), (contract_b,)), ((), ())),
        precision=HIGH, preferred_element_type=jnp.float32,
    )


def split(a):
    high = a.astype(jnp.bfloat16)
    return high, (a - high.astype(jnp.float32)).astype(jnp.bfloat16)


def dot_split(a, b, contract_a, contract_b):
    (a_high, a_low), (b_high, b_low) = a, b

    def product(left, right):
        return lax.dot_general(
            left, right, (((contract_a,), (contract_b,)), ((), ())),
            preferred_element_type=jnp.float32,
        )

    return product(a_high, b_high) + (product(a_high, b_low) + product(a_low, b_high))


def pack_body(items, counts, out):
    out[0:OWN, :] = items[...]
    priors = jnp.log(1.0 + counts[...].astype(jnp.float32))
    out[OWN:PACK, :] = jnp.zeros((PACK - OWN, E), jnp.float32)
    out[OWN:OWN + 1, 0:OWN] = priors


def column_of(row):
    size = row.shape[1]
    eye = lax.broadcasted_iota(jnp.int32, (size, size), 0) == lax.broadcasted_iota(
        jnp.int32, (size, size), 1
    )
    return jnp.sum(jnp.where(eye, jnp.broadcast_to(row, (size, size)), 0.0), axis=1, keepdims=True)


def member_of(place, k):
    core = place[2] if k < Z else 1 - place[2]
    return k % Z * CORES + core


def hits(place, positive, k):
    rows = lax.broadcasted_iota(jnp.int32, (OWN, ROWS), 0)
    return rows == positive - (place[0] * SLAB + member_of(place, k) * OWN)


def score_body(place, users, packed, positive, items, scores, stats):
    priors = []
    for k in range(MEMBERS):
        first = pl.multiple_of(member_of(place, k) * PACK, 8)
        items[OWN * k:OWN * (k + 1), :] = packed[pl.ds(first, OWN), :]
        priors.append(column_of(packed[pl.ds(first + OWN, 8), :][0:1, 0:OWN]))
    raw = dot(items[...], users[...], 1, 1)
    wanted = positive[...]
    highest = None
    picked = jnp.zeros((OWN, ROWS), jnp.float32)
    for k in range(MEMBERS):
        at = slice(OWN * k, OWN * (k + 1))
        block = raw[at, :] - priors[k]
        scores[at, :] = block
        top = jnp.max(block, axis=0, keepdims=True)
        highest = top if k == 0 else jnp.maximum(highest, top)
        picked = picked + jnp.where(hits(place, wanted, k), block, 0.0)
    total = jnp.sum(jnp.exp(scores[...] - highest), axis=0, keepdims=True)
    level = highest + jnp.log(total)
    picked = jnp.sum(picked, axis=0, keepdims=True)
    for k in range(4):
        lanes = slice(128 * k, 128 * (k + 1))
        stats[0, k:k + 1, :] = level[:, lanes]
        stats[0, 4 + k:5 + k, :] = picked[:, lanes]
    one = stats[0, :, :]
    for d in range(1, GROUPS):
        stats[d, :, :] = one


def user_body(place, items, positive, scores, stats, loss, grad, user_part, block, sent):
    highest = stats[0, 0:4, :]
    for d in range(1, GROUPS):
        highest = jnp.maximum(highest, stats[d, 0:4, :])
    total = jnp.zeros((4, 128), jnp.float32)
    picked = jnp.zeros((4, 128), jnp.float32)
    for d in range(GROUPS):
        total = total + jnp.exp(stats[d, 0:4, :] - highest)
        picked = picked + stats[d, 4:8, :]
    above = jnp.log(total)
    loss[...] = (highest + above) - picked
    base = jnp.concatenate([highest[k:k + 1, :] for k in range(4)], axis=1)
    above = jnp.concatenate([above[k:k + 1, :] for k in range(4)], axis=1)
    wanted = positive[...]
    for k in range(MEMBERS):
        at = slice(OWN * k, OWN * (k + 1))
        hit = hits(place, wanted, k)
        grad[at, :] = jnp.exp((scores[at, :] - base) - above) - jnp.where(hit, 1.0, 0.0)
    right = split(items[...])
    copies = []
    for k in range(4):
        at = pl.ds(128 * k, 128)
        block[at, :] = dot_split(split(grad[:, 128 * k:128 * (k + 1)]), right, 0, 0)
        copies.append(pltpu.make_async_copy(block.at[at, :], user_part.at[at, :], sent.at[k]))
        copies[-1].start()
    for copy in copies:
        copy.wait()


def item_body(users, grad, mine, theirs):
    right = split(users[...])
    theirs[...] = dot_split(split(grad[HALF:SLAB, :]), right, 1, 0)
    mine[...] = dot_split(split(grad[0:HALF, :]), right, 1, 0)


def add_spread_body(parts, out, block, sent):
    total = parts[0]
    for r in range(1, parts.shape[0]):
        total = total + parts[r]
    block[...] = total
    copies = [pltpu.make_async_copy(block, out.at[d], sent.at[d]) for d in range(GROUPS)]
    for copy in copies:
        copy.start()
    for copy in copies:
        copy.wait()


def halve_body(place, a, b, keep, send):
    bit = lax.rem(place[1], 2)
    for k in range(keep.shape[0] // OWN):
        at = slice(OWN * k, OWN * (k + 1))
        here = pl.ds(pl.multiple_of((2 * k + bit) * OWN, OWN), OWN)
        there = pl.ds(pl.multiple_of((2 * k + 1 - bit) * OWN, OWN), OWN)
        send[at, :] = a[there, :] + b[there, :]
        keep[at, :] = a[here, :] + b[here, :]


def deal_body(place, a, b, *outs):
    for r, out in enumerate(outs):
        pair = lax.rem(lax.shift_right_logical(place[1], 1) + r, Z // 2)
        rows = pl.ds(pl.multiple_of(pair * OWN, OWN), OWN)
        out[...] = a[rows, :] + b[rows, :]


def finish_body(user_rows, *refs):
    terms, (item_grad, user_grad, sent) = refs[:-3], refs[-3:]
    copies = []
    for k in range(8):
        at = pl.ds(ROWS // 8 * k, ROWS // 8)
        copies.append(pltpu.make_async_copy(user_rows.at[at, :], user_grad.at[at, :], sent.at[k]))
        copies[-1].start()
    total = terms[0][...]
    for ref in terms[1:]:
        total = total + ref[...]
    item_grad[...] = total
    for copy in copies:
        copy.wait()


def exchange(value, axis):
    return lax.all_to_all(value, axis, split_axis=0, concat_axis=0, tiled=True)


def move(value, target):
    pairs = []
    for z in range(Z):
        for c in range(CORES):
            z_to, c_to = target(z, c)
            pairs.append((z * CORES + c, z_to % Z * CORES + c_to))
    return lax.ppermute(value, USER_AXES, pairs)


def per_device(user_vectors, item_vectors, item_counts, positive_ids):
    place = jnp.stack([lax.axis_index(("x", "y")), lax.axis_index("z"), lax.axis_index("core")])
    place = place.astype(jnp.int32)
    positive = positive_ids.reshape(1, ROWS)
    product = 2 * ROWS * SLAB * E

    packed = call(pack_body, f32(PACK, E), (item_vectors, item_counts.reshape(1, OWN)))
    packed = lax.all_gather(packed, USER_AXES, axis=0, tiled=True)
    items, scores, stats = call(
        score_body, (f32(SLAB, E), f32(SLAB, ROWS), f32(GROUPS, 8, 128)),
        (place, user_vectors, packed, positive), scalars=1, flops=product,
    )
    stats = exchange(stats, PEERS)
    loss, grad, user_part = call(
        user_body, (f32(4, 128), f32(SLAB, ROWS), f32(ROWS, E)),
        (place, items, positive, scores, stats), scalars=1, flops=product, far=(2,),
        scratch=[pltpu.VMEM((ROWS, E), jnp.float32), pltpu.SemaphoreType.DMA((4,))],
    )
    parts = exchange(user_part.reshape(GROUPS, SHARE, E), PEERS)
    mine, theirs = call(item_body, (f32(HALF, E), f32(HALF, E)), (user_vectors, grad), flops=product)
    arrived = move(theirs, lambda z, c: (z, 1 - c))
    mine, theirs = call(
        halve_body, [f32(HALF // 2, E)] * 2, (place, mine, arrived), scalars=1,
    )
    arrived = move(theirs, lambda z, c: (z ^ 1, c))
    pieces = call(
        deal_body, [f32(OWN, E)] * (Z // 2), (place, mine, arrived), scalars=1,
    )
    spread = call(
        add_spread_body, f32(GROUPS, SHARE, E), (parts,), after=(pieces[0],), far=(0,),
        scratch=[pltpu.VMEM((SHARE, E), jnp.float32), pltpu.SemaphoreType.DMA((GROUPS,))],
    )
    user_rows = exchange(spread, PEERS).reshape(ROWS, E)
    terms = [pieces[0]]
    for r in (2, 1, 3):
        terms.append(move(pieces[r], lambda z, c, r=r: (z + 2 * r, c)))
    item_grad, user_grad = pl.pallas_call(
        finish_body,
        out_shape=(f32(OWN, E), f32(ROWS, E)),
        in_specs=[pl.BlockSpec(memory_space=pl.ANY)] + [vmem()] * len(terms),
        out_specs=(vmem(), pl.BlockSpec(memory_space=pl.ANY)),
        scratch_shapes=[pltpu.SemaphoreType.DMA((8,))],
        compiler_params=pltpu.CompilerParams(vmem_limit_bytes=VMEM_LIMIT),
    )(user_rows, *terms)
    return (loss.reshape(ROWS), user_grad, item_grad)


def solution(mesh):
    fine = Mesh(mesh.devices.reshape(X, Y, Z, CORES), ("x", "y") + USER_AXES)
    users, everything = P(USER_AXES), P(("x", "y") + USER_AXES)
    return jax.shard_map(
        per_device,
        mesh=fine,
        in_specs=(users, everything, everything, users),
        out_specs=(users, users, everything),
        check_vma=False,
    )
```

```python
import jax
import jax.numpy as jnp
from jax import lax
from jax.experimental import pallas as pl
from jax.experimental.pallas import tpu as pltpu
from jax.sharding import Mesh, PartitionSpec as P

HIGH = lax.Precision.HIGHEST
X, Y, Z, CORES = 4, 8, 8, 2
GROUPS, MEMBERS = X * Y, Z * CORES
PEERS = ("y", "x")
USER_AXES = ("z", "core")
E = 256
OWN = 32
PACK = OWN + 8
SLAB = MEMBERS * OWN
HALF = SLAB // CORES
ROWS = 512
SHARE = ROWS // GROUPS
VMEM_LIMIT = 48 * 1024 * 1024


def vmem():
    return pl.BlockSpec(memory_space=pltpu.VMEM)


def smem():
    return pl.BlockSpec(memory_space=pltpu.SMEM)


def f32(*shape):
    return jax.ShapeDtypeStruct(shape, jnp.float32)


def call(body, out_shape, operands, scalars=0, scratch=(), flops=0, after=()):
    single = not isinstance(out_shape, (tuple, list))
    outs = [out_shape] if single else list(out_shape)
    size = sum(o.size * 4 for o in operands) + sum(4 * s.size for s in outs)
    last = len(operands)
    result = pl.pallas_call(
        (lambda *refs: body(*refs[:last], *refs[last + len(after):])) if after else body,
        out_shape=outs,
        in_specs=[smem()] * scalars + [vmem()] * (len(operands) - scalars)
        + [pl.BlockSpec(memory_space=pl.ANY)] * len(after),
        out_specs=[vmem()] * len(outs),
        scratch_shapes=list(scratch),
        compiler_params=pltpu.CompilerParams(vmem_limit_bytes=VMEM_LIMIT),
        cost_estimate=pl.CostEstimate(flops=flops, bytes_accessed=size, transcendentals=0),
    )(*operands, *after)
    return result[0] if single else result


def dot(a, b, contract_a, contract_b):
    return lax.dot_general(
        a, b, (((contract_a,), (contract_b,)), ((), ())),
        precision=HIGH, preferred_element_type=jnp.float32,
    )


def split(a):
    high = a.astype(jnp.bfloat16)
    return high, (a - high.astype(jnp.float32)).astype(jnp.bfloat16)


def dot_split(a, b, contract_a, contract_b):
    (a_high, a_low), (b_high, b_low) = a, b

    def product(left, right):
        return lax.dot_general(
            left, right, (((contract_a,), (contract_b,)), ((), ())),
            preferred_element_type=jnp.float32,
        )

    return product(a_high, b_high) + (product(a_high, b_low) + product(a_low, b_high))


def pack_body(items, counts, out):
    out[0:OWN, :] = items[...]
    priors = jnp.log(1.0 + counts[...].astype(jnp.float32))
    out[OWN:PACK, :] = jnp.zeros((PACK - OWN, E), jnp.float32)
    out[OWN:OWN + 1, 0:OWN] = priors


def column_of(row):
    size = row.shape[1]
    eye = lax.broadcasted_iota(jnp.int32, (size, size), 0) == lax.broadcasted_iota(
        jnp.int32, (size, size), 1
    )
    return jnp.sum(jnp.where(eye, jnp.broadcast_to(row, (size, size)), 0.0), axis=1, keepdims=True)


def member_of(place, k):
    core = place[2] if k < Z else 1 - place[2]
    return k % Z * CORES + core


def hits(place, positive, k):
    rows = lax.broadcasted_iota(jnp.int32, (OWN, ROWS), 0)
    return rows == positive - (place[0] * SLAB + member_of(place, k) * OWN)


def score_body(place, users, packed, positive, items, scores, stats):
    priors = []
    for k in range(MEMBERS):
        first = pl.multiple_of(member_of(place, k) * PACK, 8)
        items[OWN * k:OWN * (k + 1), :] = packed[pl.ds(first, OWN), :]
        priors.append(column_of(packed[pl.ds(first + OWN, 8), :][0:1, 0:OWN]))
    raw = dot(items[...], users[...], 1, 1)
    wanted = positive[...]
    highest = None
    picked = jnp.zeros((OWN, ROWS), jnp.float32)
    for k in range(MEMBERS):
        at = slice(OWN * k, OWN * (k + 1))
        block = raw[at, :] - priors[k]
        scores[at, :] = block
        top = jnp.max(block, axis=0, keepdims=True)
        highest = top if k == 0 else jnp.maximum(highest, top)
        picked = picked + jnp.where(hits(place, wanted, k), block, 0.0)
    total = jnp.sum(jnp.exp(scores[...] - highest), axis=0, keepdims=True)
    level = highest + jnp.log(total)
    picked = jnp.sum(picked, axis=0, keepdims=True)
    for k in range(4):
        lanes = slice(128 * k, 128 * (k + 1))
        stats[0, k:k + 1, :] = level[:, lanes]
        stats[0, 4 + k:5 + k, :] = picked[:, lanes]
    one = stats[0, :, :]
    for d in range(1, GROUPS):
        stats[d, :, :] = one


def user_body(place, items, positive, scores, stats, loss, grad, user_part):
    highest = stats[0, 0:4, :]
    for d in range(1, GROUPS):
        highest = jnp.maximum(highest, stats[d, 0:4, :])
    total = jnp.zeros((4, 128), jnp.float32)
    picked = jnp.zeros((4, 128), jnp.float32)
    for d in range(GROUPS):
        total = total + jnp.exp(stats[d, 0:4, :] - highest)
        picked = picked + stats[d, 4:8, :]
    above = jnp.log(total)
    loss[...] = (highest - picked) + above
    base = jnp.concatenate([highest[k:k + 1, :] for k in range(4)], axis=1)
    above = jnp.concatenate([above[k:k + 1, :] for k in range(4)], axis=1)
    wanted = positive[...]
    for k in range(MEMBERS):
        at = slice(OWN * k, OWN * (k + 1))
        hit = hits(place, wanted, k)
        grad[at, :] = jnp.exp((scores[at, :] - base) - above) - jnp.where(hit, 1.0, 0.0)
    user_part[...] = dot_split(split(grad[...]), split(items[...]), 0, 0)


def item_body(users, grad, mine, theirs):
    right = split(users[...])
    theirs[...] = dot_split(split(grad[HALF:SLAB, :]), right, 1, 0)
    mine[...] = dot_split(split(grad[0:HALF, :]), right, 1, 0)


def add_spread_body(parts, out):
    total = parts[0]
    for r in range(1, parts.shape[0]):
        total = total + parts[r]
    for r in range(out.shape[0]):
        out[r] = total


def halve_body(place, a, b, keep, send):
    bit = lax.rem(place[1], 2)
    for k in range(keep.shape[0] // OWN):
        at = slice(OWN * k, OWN * (k + 1))
        here = pl.ds(pl.multiple_of((2 * k + bit) * OWN, OWN), OWN)
        there = pl.ds(pl.multiple_of((2 * k + 1 - bit) * OWN, OWN), OWN)
        send[at, :] = a[there, :] + b[there, :]
        keep[at, :] = a[here, :] + b[here, :]


def deal_body(place, a, b, *outs):
    for r, out in enumerate(outs):
        pair = lax.rem(lax.shift_right_logical(place[1], 1) + r, Z // 2)
        rows = pl.ds(pl.multiple_of(pair * OWN, OWN), OWN)
        out[...] = a[rows, :] + b[rows, :]


def sum_body(*refs):
    total = refs[0][...]
    for ref in refs[1:-1]:
        total = total + ref[...]
    refs[-1][...] = total


def exchange(value, axis):
    return lax.all_to_all(value, axis, split_axis=0, concat_axis=0, tiled=True)


def move(value, target):
    pairs = []
    for z in range(Z):
        for c in range(CORES):
            z_to, c_to = target(z, c)
            pairs.append((z * CORES + c, z_to % Z * CORES + c_to))
    return lax.ppermute(value, USER_AXES, pairs)


def per_device(user_vectors, item_vectors, item_counts, positive_ids):
    place = jnp.stack([lax.axis_index(("x", "y")), lax.axis_index("z"), lax.axis_index("core")])
    place = place.astype(jnp.int32)
    positive = positive_ids.reshape(1, ROWS)
    product = 2 * ROWS * SLAB * E

    packed = call(pack_body, f32(PACK, E), (item_vectors, item_counts.reshape(1, OWN)))
    packed = lax.all_gather(packed, USER_AXES, axis=0, tiled=True)
    items, scores, stats = call(
        score_body, (f32(SLAB, E), f32(SLAB, ROWS), f32(GROUPS, 8, 128)),
        (place, user_vectors, packed, positive), scalars=1, flops=product,
    )
    stats = exchange(stats, PEERS)
    loss, grad, user_part = call(
        user_body, (f32(4, 128), f32(SLAB, ROWS), f32(ROWS, E)),
        (place, items, positive, scores, stats), scalars=1, flops=product,
    )
    parts = exchange(user_part.reshape(GROUPS, SHARE, E), PEERS)
    mine, theirs = call(item_body, (f32(HALF, E), f32(HALF, E)), (user_vectors, grad), flops=product)
    arrived = move(theirs, lambda z, c: (z, 1 - c))
    mine, theirs = call(
        halve_body, [f32(HALF // 2, E)] * 2, (place, mine, arrived), scalars=1,
    )
    arrived = move(theirs, lambda z, c: (z ^ 1, c))
    pieces = call(
        deal_body, [f32(OWN, E)] * (Z // 2), (place, mine, arrived), scalars=1,
    )
    spread = call(add_spread_body, f32(GROUPS, SHARE, E), (parts,), after=(pieces[0],))
    user_grad = exchange(spread, PEERS).reshape(ROWS, E)
    terms = [pieces[0]]
    for r in (2, 1, 3):
        terms.append(move(pieces[r], lambda z, c, r=r: (z + 2 * r, c)))
    item_grad = call(sum_body, f32(OWN, E), terms)
    return (loss.reshape(ROWS), user_grad, item_grad)


def solution(mesh):
    fine = Mesh(mesh.devices.reshape(X, Y, Z, CORES), ("x", "y") + USER_AXES)
    users, everything = P(USER_AXES), P(("x", "y") + USER_AXES)
    return jax.shard_map(
        per_device,
        mesh=fine,
        in_specs=(users, everything, everything, users),
        out_specs=(users, users, everything),
        check_vma=False,
    )
```

```python
import functools

import jax
import jax.numpy as jnp
from jax import lax
from jax.experimental import pallas as pl
from jax.experimental.pallas import tpu as pltpu
from jax.sharding import Mesh, PartitionSpec as P

HIGH = lax.Precision.HIGHEST
X, Y, Z, CORES = 4, 8, 8, 2
GROUPS, MEMBERS = X * Y, Z * CORES
PEERS = ("y", "x")
USER_AXES = ("z", "core")
E = 256
OWN = 32
PACK = OWN + 8
SLAB = MEMBERS * OWN
HALF = SLAB // CORES
ROWS = 512
SHARE = ROWS // GROUPS
VMEM_LIMIT = 48 * 1024 * 1024


def vmem():
    return pl.BlockSpec(memory_space=pltpu.VMEM)


def smem():
    return pl.BlockSpec(memory_space=pltpu.SMEM)


def f32(*shape):
    return jax.ShapeDtypeStruct(shape, jnp.float32)


def call(body, out_shape, operands, scalars=0, scratch=(), flops=0, after=()):
    single = not isinstance(out_shape, (tuple, list))
    outs = [out_shape] if single else list(out_shape)
    size = sum(o.size * 4 for o in operands) + sum(4 * s.size for s in outs)
    last = len(operands)
    result = pl.pallas_call(
        (lambda *refs: body(*refs[:last], *refs[last + len(after):])) if after else body,
        out_shape=outs,
        in_specs=[smem()] * scalars + [vmem()] * (len(operands) - scalars)
        + [pl.BlockSpec(memory_space=pl.ANY)] * len(after),
        out_specs=[vmem()] * len(outs),
        scratch_shapes=list(scratch),
        compiler_params=pltpu.CompilerParams(vmem_limit_bytes=VMEM_LIMIT),
        cost_estimate=pl.CostEstimate(flops=flops, bytes_accessed=size, transcendentals=0),
    )(*operands, *after)
    return result[0] if single else result


def dot(a, b, contract_a, contract_b):
    return lax.dot_general(
        a, b, (((contract_a,), (contract_b,)), ((), ())),
        precision=HIGH, preferred_element_type=jnp.float32,
    )


def split(a):
    high = a.astype(jnp.bfloat16)
    return high, (a - high.astype(jnp.float32)).astype(jnp.bfloat16)


def dot_split(a, b, contract_a, contract_b):
    (a_high, a_low), (b_high, b_low) = a, b

    def product(left, right):
        return lax.dot_general(
            left, right, (((contract_a,), (contract_b,)), ((), ())),
            preferred_element_type=jnp.float32,
        )

    return product(a_high, b_high) + (product(a_high, b_low) + product(a_low, b_high))


def pack_body(items, counts, out):
    out[0:OWN, :] = items[...]
    priors = jnp.log(1.0 + counts[...].astype(jnp.float32))
    out[OWN:PACK, :] = jnp.zeros((PACK - OWN, E), jnp.float32)
    out[OWN:OWN + 1, 0:OWN] = priors


def column_of(row):
    size = row.shape[1]
    eye = lax.broadcasted_iota(jnp.int32, (size, size), 0) == lax.broadcasted_iota(
        jnp.int32, (size, size), 1
    )
    return jnp.sum(jnp.where(eye, jnp.broadcast_to(row, (size, size)), 0.0), axis=1, keepdims=True)


def member_of(place, k):
    core = place[2] if k < Z else 1 - place[2]
    return k % Z * CORES + core


def hits(place, positive, k):
    rows = lax.broadcasted_iota(jnp.int32, (OWN, ROWS), 0)
    return rows == positive - (place[0] * SLAB + member_of(place, k) * OWN)


def score_body(place, users, packed, positive, items, scores, stats):
    priors = []
    for k in range(MEMBERS):
        first = pl.multiple_of(member_of(place, k) * PACK, 8)
        items[OWN * k:OWN * (k + 1), :] = packed[pl.ds(first, OWN), :]
        priors.append(column_of(packed[pl.ds(first + OWN, 8), :][0:1, 0:OWN]))
    raw = dot(items[...], users[...], 1, 1)
    wanted = positive[...]
    highest = None
    picked = jnp.zeros((OWN, ROWS), jnp.float32)
    for k in range(MEMBERS):
        at = slice(OWN * k, OWN * (k + 1))
        block = raw[at, :] - priors[k]
        scores[at, :] = block
        top = jnp.max(block, axis=0, keepdims=True)
        highest = top if k == 0 else jnp.maximum(highest, top)
        picked = picked + jnp.where(hits(place, wanted, k), block, 0.0)
    total = jnp.sum(jnp.exp(scores[...] - highest), axis=0, keepdims=True)
    level = highest + jnp.log(total)
    picked = jnp.sum(picked, axis=0, keepdims=True)
    for k in range(4):
        lanes = slice(128 * k, 128 * (k + 1))
        stats[0, k:k + 1, :] = level[:, lanes]
        stats[0, 4 + k:5 + k, :] = picked[:, lanes]
    one = stats[0, :, :]
    for d in range(1, GROUPS):
        stats[d, :, :] = one


def user_body(place, items, positive, scores, stats, loss, grad, user_part):
    highest = stats[0, 0:4, :]
    for d in range(1, GROUPS):
        highest = jnp.maximum(highest, stats[d, 0:4, :])
    total = jnp.zeros((4, 128), jnp.float32)
    picked = jnp.zeros((4, 128), jnp.float32)
    for d in range(GROUPS):
        total = total + jnp.exp(stats[d, 0:4, :] - highest)
        picked = picked + stats[d, 4:8, :]
    above = jnp.log(total)
    loss[...] = (highest - picked) + above
    base = jnp.concatenate([highest[k:k + 1, :] for k in range(4)], axis=1)
    above = jnp.concatenate([above[k:k + 1, :] for k in range(4)], axis=1)
    wanted = positive[...]
    for k in range(MEMBERS):
        at = slice(OWN * k, OWN * (k + 1))
        hit = hits(place, wanted, k)
        grad[at, :] = jnp.exp((scores[at, :] - base) - above) - jnp.where(hit, 1.0, 0.0)
    user_part[...] = dot_split(split(grad[...]), split(items[...]), 0, 0)


def item_body(part, users, grad, out):
    rows = grad[HALF * part:HALF * (part + 1), :]
    out[...] = dot_split(split(rows), split(users[...]), 1, 0)


def add_spread_body(parts, out):
    total = parts[0]
    for r in range(1, parts.shape[0]):
        total = total + parts[r]
    for r in range(out.shape[0]):
        out[r] = total


def halve_body(place, a, b, keep, send):
    bit = lax.rem(place[1], 2)
    for k in range(keep.shape[0] // OWN):
        at = slice(OWN * k, OWN * (k + 1))
        here = pl.ds(pl.multiple_of((2 * k + bit) * OWN, OWN), OWN)
        there = pl.ds(pl.multiple_of((2 * k + 1 - bit) * OWN, OWN), OWN)
        send[at, :] = a[there, :] + b[there, :]
        keep[at, :] = a[here, :] + b[here, :]


def deal_body(place, a, b, *outs):
    for r, out in enumerate(outs):
        pair = lax.rem(lax.shift_right_logical(place[1], 1) + r, Z // 2)
        rows = pl.ds(pl.multiple_of(pair * OWN, OWN), OWN)
        out[...] = a[rows, :] + b[rows, :]


def sum_body(*refs):
    total = refs[0][...]
    for ref in refs[1:-1]:
        total = total + ref[...]
    refs[-1][...] = total


def exchange(value, axis):
    return lax.all_to_all(value, axis, split_axis=0, concat_axis=0, tiled=True)


def move(value, target):
    pairs = []
    for z in range(Z):
        for c in range(CORES):
            z_to, c_to = target(z, c)
            pairs.append((z * CORES + c, z_to % Z * CORES + c_to))
    return lax.ppermute(value, USER_AXES, pairs)


def per_device(user_vectors, item_vectors, item_counts, positive_ids):
    place = jnp.stack([lax.axis_index(("x", "y")), lax.axis_index("z"), lax.axis_index("core")])
    place = place.astype(jnp.int32)
    positive = positive_ids.reshape(1, ROWS)
    product = 2 * ROWS * SLAB * E

    packed = call(pack_body, f32(PACK, E), (item_vectors, item_counts.reshape(1, OWN)))
    packed = lax.all_gather(packed, USER_AXES, axis=0, tiled=True)
    items, scores, stats = call(
        score_body, (f32(SLAB, E), f32(SLAB, ROWS), f32(GROUPS, 8, 128)),
        (place, user_vectors, packed, positive), scalars=1, flops=product,
    )
    stats = exchange(stats, PEERS)
    loss, grad, user_part = call(
        user_body, (f32(4, 128), f32(SLAB, ROWS), f32(ROWS, E)),
        (place, items, positive, scores, stats), scalars=1, flops=product,
    )
    parts = exchange(user_part.reshape(GROUPS, SHARE, E), PEERS)
    mine, theirs = (
        call(functools.partial(item_body, part), f32(HALF, E), (user_vectors, grad), flops=product // 2)
        for part in range(2)
    )
    arrived = move(theirs, lambda z, c: (z, 1 - c))
    mine, theirs = call(
        halve_body, [f32(HALF // 2, E)] * 2, (place, mine, arrived), scalars=1,
    )
    arrived = move(theirs, lambda z, c: (z ^ 1, c))
    pieces = call(
        deal_body, [f32(OWN, E)] * (Z // 2), (place, mine, arrived), scalars=1,
    )
    spread = call(add_spread_body, f32(GROUPS, SHARE, E), (parts,), after=(pieces[0],))
    user_grad = exchange(spread, PEERS).reshape(ROWS, E)
    terms = [pieces[0]]
    for r in (2, 1, 3):
        terms.append(move(pieces[r], lambda z, c, r=r: (z + 2 * r, c)))
    item_grad = call(sum_body, f32(OWN, E), terms)
    return (loss.reshape(ROWS), user_grad, item_grad)


def solution(mesh):
    fine = Mesh(mesh.devices.reshape(X, Y, Z, CORES), ("x", "y") + USER_AXES)
    users, everything = P(USER_AXES), P(("x", "y") + USER_AXES)
    return jax.shard_map(
        per_device,
        mesh=fine,
        in_specs=(users, everything, everything, users),
        out_specs=(users, users, everything),
        check_vma=False,
    )
```

```python
import jax
import jax.numpy as jnp
from jax import lax
from jax.experimental import pallas as pl
from jax.experimental.pallas import tpu as pltpu
from jax.sharding import Mesh, PartitionSpec as P

HIGH = lax.Precision.HIGHEST
X, Y, Z, CORES = 4, 8, 8, 2
GROUPS, MEMBERS = X * Y, Z * CORES
PEERS = ("y", "x")
USER_AXES = ("z", "core")
E = 256
OWN = 32
PACK = OWN + 8
SLAB = MEMBERS * OWN
HALF = SLAB // CORES
ROWS = 512
SHARE = ROWS // GROUPS
VMEM_LIMIT = 48 * 1024 * 1024


def vmem():
    return pl.BlockSpec(memory_space=pltpu.VMEM)


def smem():
    return pl.BlockSpec(memory_space=pltpu.SMEM)


def f32(*shape):
    return jax.ShapeDtypeStruct(shape, jnp.float32)


def call(body, out_shape, operands, scalars=0, scratch=(), flops=0, after=()):
    single = not isinstance(out_shape, (tuple, list))
    outs = [out_shape] if single else list(out_shape)
    size = sum(o.size * 4 for o in operands) + sum(4 * s.size for s in outs)
    last = len(operands)
    result = pl.pallas_call(
        (lambda *refs: body(*refs[:last], *refs[last + len(after):])) if after else body,
        out_shape=outs,
        in_specs=[smem()] * scalars + [vmem()] * (len(operands) - scalars)
        + [pl.BlockSpec(memory_space=pl.ANY)] * len(after),
        out_specs=[vmem()] * len(outs),
        scratch_shapes=list(scratch),
        compiler_params=pltpu.CompilerParams(vmem_limit_bytes=VMEM_LIMIT),
        cost_estimate=pl.CostEstimate(flops=flops, bytes_accessed=size, transcendentals=0),
    )(*operands, *after)
    return result[0] if single else result


def dot(a, b, contract_a, contract_b):
    return lax.dot_general(
        a, b, (((contract_a,), (contract_b,)), ((), ())),
        precision=HIGH, preferred_element_type=jnp.float32,
    )


def split(a):
    high = a.astype(jnp.bfloat16)
    return high, (a - high.astype(jnp.float32)).astype(jnp.bfloat16)


def dot_split(a, b, contract_a, contract_b):
    (a_high, a_low), (b_high, b_low) = a, b

    def product(left, right):
        return lax.dot_general(
            left, right, (((contract_a,), (contract_b,)), ((), ())),
            preferred_element_type=jnp.float32,
        )

    return product(a_high, b_high) + (product(a_high, b_low) + product(a_low, b_high))


def pack_body(items, counts, out):
    out[0:OWN, :] = items[...]
    priors = jnp.log(1.0 + counts[...].astype(jnp.float32))
    out[OWN:PACK, :] = jnp.zeros((PACK - OWN, E), jnp.float32)
    out[OWN:OWN + 1, 0:OWN] = priors


def column_of(row):
    size = row.shape[1]
    eye = lax.broadcasted_iota(jnp.int32, (size, size), 0) == lax.broadcasted_iota(
        jnp.int32, (size, size), 1
    )
    return jnp.sum(jnp.where(eye, jnp.broadcast_to(row, (size, size)), 0.0), axis=1, keepdims=True)


def member_of(place, k):
    core = place[2] if k < Z else 1 - place[2]
    return k % Z * CORES + core


def hits(place, positive, k):
    rows = lax.broadcasted_iota(jnp.int32, (OWN, ROWS), 0)
    return rows == positive - (place[0] * SLAB + member_of(place, k) * OWN)


def score_body(place, users, packed, positive, items, scores, stats):
    priors = []
    for k in range(MEMBERS):
        first = pl.multiple_of(member_of(place, k) * PACK, 8)
        items[OWN * k:OWN * (k + 1), :] = packed[pl.ds(first, OWN), :]
        priors.append(column_of(packed[pl.ds(first + OWN, 8), :][0:1, 0:OWN]))
    raw = dot(items[...], users[...], 1, 1)
    wanted = positive[...]
    highest = None
    picked = jnp.zeros((OWN, ROWS), jnp.float32)
    for k in range(MEMBERS):
        at = slice(OWN * k, OWN * (k + 1))
        block = raw[at, :] - priors[k]
        scores[at, :] = block
        top = jnp.max(block, axis=0, keepdims=True)
        highest = top if k == 0 else jnp.maximum(highest, top)
        picked = picked + jnp.where(hits(place, wanted, k), block, 0.0)
    total = jnp.sum(jnp.exp(scores[...] - highest), axis=0, keepdims=True)
    level = highest + jnp.log(total)
    picked = jnp.sum(picked, axis=0, keepdims=True)
    for k in range(4):
        lanes = slice(128 * k, 128 * (k + 1))
        stats[0, k:k + 1, :] = level[:, lanes]
        stats[0, 4 + k:5 + k, :] = picked[:, lanes]
    one = stats[0, :, :]
    for d in range(1, GROUPS):
        stats[d, :, :] = one


def user_body(place, items, positive, scores, stats, loss, grad, user_part):
    highest = stats[0, 0:4, :]
    for d in range(1, GROUPS):
        highest = jnp.maximum(highest, stats[d, 0:4, :])
    total = jnp.zeros((4, 128), jnp.float32)
    picked = jnp.zeros((4, 128), jnp.float32)
    for d in range(GROUPS):
        total = total + jnp.exp(stats[d, 0:4, :] - highest)
        picked = picked + stats[d, 4:8, :]
    above = jnp.log(total)
    loss[...] = (highest - picked) + above
    base = jnp.concatenate([highest[k:k + 1, :] for k in range(4)], axis=1)
    above = jnp.concatenate([above[k:k + 1, :] for k in range(4)], axis=1)
    wanted = positive[...]
    for k in range(MEMBERS):
        at = slice(OWN * k, OWN * (k + 1))
        hit = hits(place, wanted, k)
        grad[at, :] = jnp.exp((scores[at, :] - base) - above) - jnp.where(hit, 1.0, 0.0)
    user_part[...] = dot_split(split(grad[...]), split(items[...]), 0, 0)


def item_body(users, grad, mine, theirs):
    right = split(users[...])
    theirs[...] = dot_split(split(grad[HALF:SLAB, :]), right, 1, 0)
    mine[...] = dot_split(split(grad[0:HALF, :]), right, 1, 0)


def add_spread_body(parts, out):
    total = parts[0]
    for r in range(1, parts.shape[0]):
        total = total + parts[r]
    for r in range(out.shape[0]):
        out[r] = total


def halve_body(place, a, b, keep, send):
    bit = lax.rem(place[1], 2)
    for k in range(keep.shape[0] // OWN):
        at = slice(OWN * k, OWN * (k + 1))
        here = pl.ds(pl.multiple_of((2 * k + bit) * OWN, OWN), OWN)
        there = pl.ds(pl.multiple_of((2 * k + 1 - bit) * OWN, OWN), OWN)
        send[at, :] = a[there, :] + b[there, :]
        keep[at, :] = a[here, :] + b[here, :]


def deal_body(place, a, b, *outs):
    for r, out in enumerate(outs):
        pair = lax.rem(lax.shift_right_logical(place[1], 1) + r, Z // 2)
        rows = pl.ds(pl.multiple_of(pair * OWN, OWN), OWN)
        out[...] = a[rows, :] + b[rows, :]


def sum_body(*refs):
    total = refs[0][...]
    for ref in refs[1:-1]:
        total = total + ref[...]
    refs[-1][...] = total


def exchange(value, axis):
    return lax.all_to_all(value, axis, split_axis=0, concat_axis=0, tiled=True)


def move(value, target):
    pairs = []
    for z in range(Z):
        for c in range(CORES):
            z_to, c_to = target(z, c)
            pairs.append((z * CORES + c, z_to % Z * CORES + c_to))
    return lax.ppermute(value, USER_AXES, pairs)


def per_device(user_vectors, item_vectors, item_counts, positive_ids):
    place = jnp.stack([lax.axis_index(("x", "y")), lax.axis_index("z"), lax.axis_index("core")])
    place = place.astype(jnp.int32)
    positive = positive_ids.reshape(1, ROWS)
    product = 2 * ROWS * SLAB * E

    packed = call(pack_body, f32(PACK, E), (item_vectors, item_counts.reshape(1, OWN)))
    packed = lax.all_gather(packed, USER_AXES, axis=0, tiled=True)
    items, scores, stats = call(
        score_body, (f32(SLAB, E), f32(SLAB, ROWS), f32(GROUPS, 8, 128)),
        (place, user_vectors, packed, positive), scalars=1, flops=product,
    )
    stats = exchange(stats, PEERS)
    loss, grad, user_part = call(
        user_body, (f32(4, 128), f32(SLAB, ROWS), f32(ROWS, E)),
        (place, items, positive, scores, stats), scalars=1, flops=product,
    )
    parts = exchange(user_part.reshape(GROUPS, SHARE, E), PEERS)
    mine, theirs = call(item_body, (f32(HALF, E), f32(HALF, E)), (user_vectors, grad), flops=product)
    arrived = move(theirs, lambda z, c: (z, 1 - c))
    mine, theirs = call(
        halve_body, [f32(HALF // 2, E)] * 2, (place, mine, arrived), scalars=1,
    )
    arrived = move(theirs, lambda z, c: (z ^ 1, c))
    pieces = call(
        deal_body, [f32(OWN, E)] * (Z // 2), (place, mine, arrived), scalars=1,
    )
    spread = call(add_spread_body, f32(GROUPS, SHARE, E), (parts,), after=(arrived,))
    user_grad = exchange(spread, PEERS).reshape(ROWS, E)
    terms = [pieces[0]]
    for r in (2, 1, 3):
        terms.append(move(pieces[r], lambda z, c, r=r: (z + 2 * r, c)))
    item_grad = call(sum_body, f32(OWN, E), terms)
    return (loss.reshape(ROWS), user_grad, item_grad)


def solution(mesh):
    fine = Mesh(mesh.devices.reshape(X, Y, Z, CORES), ("x", "y") + USER_AXES)
    users, everything = P(USER_AXES), P(("x", "y") + USER_AXES)
    return jax.shard_map(
        per_device,
        mesh=fine,
        in_specs=(users, everything, everything, users),
        out_specs=(users, users, everything),
        check_vma=False,
    )
```
